32 devices in a mesh: prow: 4 (over y, x), pcol: 8 (over z, core).
Axes of the slice: x: 2, y: 2, z: 4, core: 2. Of those that a mesh axis runs over, the one named last changes fastest.
Arguments:
- ainv: float32 [16384, 16384], P('prow', 'pcol'), as said below
- panels: float32 [3, 16384, 512], P(None, 'prow', 'pcol'), may hold values from -0.53 to 0.53
- pattern: int32 [3, 128], replicated, may hold values 0 or 1
- coupling: float32 [3, 512, 512], replicated, may hold values from -0.25 to 0.25
- dinv: float32 [3, 512, 512], replicated, as said below
Outputs:
- xpanel: float32 [3, 16384, 512], P(None, 'prow', 'pcol')
- xcross: float32 [3, 512, 512], P(None, 'pcol')
- ydiag: float32 [3, 512, 512], P(None, 'pcol')
The draws below stay inside these ranges and needn't reach their ends.
Inputs may be any that keep to these rules, and one draw needn't show every extreme that they name: ainv is symmetric: ainv equals its transpose up to rounding. Each dinv[k] is symmetric: it equals its transpose exactly.
All inputs are finite; a program needn't handle non-finite values.
Results may differ from the reference program's by a relative error of at most 0.000092.
Values sent between devices are 32-bit elements; how exact they have to be, the bound alone decides.
No kernel may reach another device: no remote copies, remote signals or barrier semaphores. Data moves between devices by JAX's collectives and lax.ppermute only.
A program may use at most 192 MiB of HBM per device.

```python
import jax
import jax.numpy as jnp
from jax import lax

NB = 128
W = 512
M = 16384
NBLK = 128


def draw_ainv(key, part):
    sample = jax.random.normal(jax.random.fold_in(key, 11), (M, M), jnp.float32)
    symmetric = (sample + sample.T) * 0.5 ** 0.5
    return jnp.clip(symmetric, -6.0, 6.0) * M ** (-0.5)


def draw_dinv(key, part):
    sample = jax.random.normal(jax.random.fold_in(key, 22), (3, W, W), jnp.float32) * 0.5
    symmetric = (sample + jnp.swapaxes(sample, 1, 2)) * 0.5 ** 0.5
    return jnp.clip(symmetric, -3.0, 3.0)


def set_ends(array, key, low, top_value):
    longest = array.shape.index(max(array.shape))
    spots = []
    for shift in (0, 1):
        where = [jax.random.randint(jax.random.fold_in(key, axis), (), 0, length) for axis, length in enumerate(array.shape)]
        where[longest] = (where[longest] + shift) % array.shape[longest]
        spots.append(tuple(where))
    return array.at[spots[0]].set(low).at[spots[1]].set(top_value)


def shard_levels(stream_key, extent, cuts, least, top_value):
    factor_of, own = 1.0, jax.random.fold_in(stream_key, 6)
    for dim, shards_of in cuts:
        draws = jnp.exp(jax.random.uniform(jax.random.fold_in(own, dim), (shards_of,), jnp.float32, least / len(cuts), top_value / len(cuts)))
        factor_of = factor_of * jnp.repeat(draws, extent[dim] // shards_of).reshape([-1 if axis == dim else 1 for axis in range(len(extent))])
    return factor_of


def gaussian(rng, dims, scale, reach, pieces=(), dtype=jnp.bfloat16):
    values = scale * jax.random.normal(rng, dims, jnp.float32)
    if pieces:
        values = values * shard_levels(rng, dims, pieces, -0.22, 0.18)
    return jnp.clip(values, -reach, reach).astype(dtype)


def setup_inputs(seed: int = 0) -> dict:
    keys = jax.random.split(jax.random.key(seed), 6)
    ainv = draw_ainv(jax.random.fold_in(keys[5], 71), 0)
    panels = gaussian(keys[1], (3, M, W), 0.088, 0.53, ((1, 4), (2, 8)), jnp.float32)
    pattern = set_ends((jax.random.randint(keys[2], (3, NBLK), 0, 4) < 3).astype(jnp.int32), jax.random.fold_in(keys[2], 1), 0, 1)
    coupling = gaussian(keys[3], (3, W, W), W ** -0.5, 0.25, (), jnp.float32)
    dinv = draw_dinv(jax.random.fold_in(keys[5], 71), 0)
    return {"ainv": ainv, "panels": panels, "pattern": pattern, "coupling": coupling, "dinv": dinv}


def matmul(left, right):
    return jnp.dot(left, right, precision=lax.Precision.HIGHEST, preferred_element_type=jnp.float32)


def tdot(left, right):
    return lax.dot_general(left, right, (((0,), (0,)), ((), ())), precision=lax.Precision.HIGHEST, preferred_element_type=jnp.float32)


def reference(ainv, panels, pattern, coupling, dinv):
    row_mask = jnp.repeat(pattern.astype(jnp.float32), NB, axis=1)
    factors = panels * row_mask[:, :, None]
    first, second, third = coupling[0], coupling[1], coupling[2]
    col_zero = -matmul(ainv, factors[0])
    col_one = -(matmul(ainv, factors[1]) + matmul(col_zero, first))
    col_two = -(matmul(ainv, factors[2]) + matmul(col_zero, second) + matmul(col_one, third))
    diag_zero = dinv[0] - tdot(factors[0], col_zero)
    cross_one = -(tdot(col_zero, factors[1]) + matmul(diag_zero, first))
    diag_one = dinv[1] - tdot(factors[1], col_one) - tdot(first, cross_one)
    cross_two = -(tdot(col_zero, factors[2]) + matmul(diag_zero, second) + matmul(cross_one, third))
    cross_three = -(tdot(col_one, factors[2]) + tdot(cross_one, second) + matmul(diag_one, third))
    diag_two = dinv[2] - tdot(factors[2], col_two) - tdot(second, cross_two) - tdot(third, cross_three)
    xpanel = jnp.stack([col_zero, col_one, col_two], 0)
    xcross = jnp.stack([cross_one, cross_two, cross_three], 0)
    ydiag = jnp.stack([diag_zero, diag_one, diag_two], 0)
    return (xpanel, xcross, ydiag)
```

```python
import jax
import jax.numpy as jnp
from jax import lax
from jax.sharding import PartitionSpec as P

NB = 128

precise = lax.Precision.HIGHEST


def matmul(left, right):
    return jnp.dot(left, right, precision=precise, preferred_element_type=jnp.float32)


def tdot(left, right, precision=precise):
    return lax.dot_general(
        left, right, (((0,), (0,)), ((), ())), precision=precision, preferred_element_type=jnp.float32
    )


def split(values):
    high = lax.reduce_precision(values, exponent_bits=8, mantissa_bits=7)
    return high.astype(jnp.bfloat16), (values - high).astype(jnp.bfloat16)


def exchange(value, axis, size, step):
    return lax.ppermute(value, axis, [(i, i ^ step) for i in range(size)])


def shards(ainv, panels, pattern, coupling, dinv):
    rows_n = lax.axis_size("prow")
    cols_n = lax.axis_size("pcol")
    row = lax.axis_index("prow")
    col = lax.axis_index("pcol")
    local_rows, local_cols = panels.shape[1:]
    width = ainv.shape[1]
    part = width // rows_n
    ratio = cols_n // rows_n
    half = local_cols // 2
    blocks_here = local_rows // NB

    flags = lax.dynamic_slice_in_dim(pattern, row * blocks_here, blocks_here, 1)
    mask = jnp.repeat(flags.astype(jnp.float32), NB, axis=1)
    shard = jnp.swapaxes(panels, 1, 2) * mask[:, None, :]

    chunks = [(0, 0, local_cols), (1, 0, local_cols), (2, 0, half), (2, half, local_cols)]
    gathered = [
        lax.all_gather(shard[j, lo:hi], "pcol", axis=0, tiled=True) for j, lo, hi in chunks
    ]

    inverse = []
    for step in range(rows_n):
        piece = lax.dynamic_slice_in_dim(ainv, (row ^ step) * part, part, 1)
        high, low = split(piece)
        inverse.append(jnp.concatenate([high, low, high], 0))

    def columns(matrix, lo, hi):
        whole = matrix.shape[0]
        return matrix.reshape(whole, cols_n, local_cols)[:, :, lo:hi].reshape(whole, -1)

    def triple(values):
        high, low = split(values)
        return jnp.concatenate([high, high, low], 1)

    high_precision = lax.Precision.HIGH
    eliminated = []
    for (j, lo, hi), value in zip(chunks, gathered):
        if j == 1:
            value = value - tdot(coupling[0], eliminated[0], high_precision)
        if j == 2:
            value = value - (
                tdot(columns(coupling[1], lo, hi), eliminated[0], high_precision)
                + tdot(columns(coupling[2], lo, hi), eliminated[1], high_precision)
            )
        eliminated.append(value)
    factors = [triple(value) for value in eliminated]

    finished = []
    for value in factors:
        products = [
            jnp.dot(value, inverse[step], preferred_element_type=jnp.float32)
            for step in range(rows_n)
        ]
        total = products[0]
        for step in range(1, rows_n):
            total = total + exchange(products[step], "prow", rows_n, step)
        count = total.shape[0] // cols_n
        moved = lax.all_to_all((-total).reshape(cols_n, count, part), "pcol", 0, 0)
        moved = lax.all_to_all(moved.reshape(rows_n, ratio, count, part), "prow", 0, 0)
        finished.append(moved.transpose(2, 1, 0, 3).reshape(count, local_rows))

    inner = [[], [], []]
    for (j, lo, hi), value in zip(chunks, finished):
        high, low = split(-value)
        left = jnp.concatenate([high, low, high], 1)
        terms = []
        for (k, first, last), right in zip(chunks, factors):
            if k < j:
                continue
            term = lax.dot_general(
                left, right, (((1,), (1,)), ((), ())), preferred_element_type=jnp.float32
            )
            terms.append(term)
        term = jnp.concatenate(terms, 1)
        summed = term
        for step in range(1, rows_n):
            summed = summed + exchange(term, "prow", rows_n, step)
        blocks = []
        for k in range(j, 3):
            pieces = []
            for k2, first, last in chunks:
                if k2 == k:
                    size = cols_n * (last - first)
                    pieces.append(summed[:, :size].reshape(hi - lo, cols_n, last - first))
                    summed = summed[:, size:]
            blocks.append(jnp.concatenate(pieces, 2).reshape(hi - lo, cols_n * local_cols))
        inner[j].append(blocks)
    inner = [[jnp.concatenate(b, 0) for b in zip(*parts)] for parts in inner]

    first, second, third = coupling[0], coupling[1], coupling[2]
    start = col * local_cols

    def own_rows(matrix):
        return lax.dynamic_slice_in_dim(matrix, start, local_cols, 0)

    def own_cols(matrix):
        return lax.dynamic_slice_in_dim(matrix, start, local_cols, 1)

    bridge = second - matmul(first, third)
    d0 = own_rows(dinv[0])
    d1 = own_rows(dinv[1])
    k0 = tdot(own_cols(first), dinv[0])
    k1 = tdot(own_cols(bridge), dinv[0])
    k2 = tdot(own_cols(third), dinv[1])
    diag_zero = d0 + inner[0][0]
    cross_one = inner[0][1] - matmul(d0, first)
    cross_two = inner[0][2] - matmul(d0, bridge)
    diag_one = inner[1][0] + (d1 + matmul(k0, first))
    cross_three = inner[1][1] + (matmul(k0, bridge) - matmul(d1, third))
    diag_two = inner[2][0] + (own_rows(dinv[2]) + matmul(k1, bridge) + matmul(k2, third))

    panel_parts = [[], [], []]
    for (j, lo, hi), value in zip(chunks, finished):
        panel_parts[j].append(value)
    xpanel = jnp.stack([jnp.concatenate(p, 0) for p in panel_parts], 0)
    xcross = jnp.stack([cross_one, cross_two, cross_three], 0)
    ydiag = jnp.stack([diag_zero, diag_one, diag_two], 0)
    return (jnp.swapaxes(xpanel, 1, 2), xcross, ydiag)


def solution(mesh):
    placed = (P("prow", "pcol"), P(None, "prow", "pcol"), P(), P(), P())
    return jax.shard_map(
        shards,
        mesh=mesh,
        in_specs=placed,
        out_specs=(P(None, "prow", "pcol"), P(None, "pcol", None), P(None, "pcol", None)),
        check_vma=False,
    )
```

```python
import functools

import jax
import jax.numpy as jnp
from jax import lax
from jax.experimental import pallas as pl
from jax.experimental.pallas import tpu as pltpu
from jax.sharding import PartitionSpec as P

NB = 128
MIB = 1024 * 1024

precise = lax.Precision.HIGHEST


def matmul(left, right):
    return jnp.dot(left, right, precision=precise, preferred_element_type=jnp.float32)


def tdot(left, right):
    return lax.dot_general(
        left, right, (((0,), (0,)), ((), ())), precision=precise, preferred_element_type=jnp.float32
    )


def tile_of(size, wanted):
    return wanted if size % wanted == 0 else size


def split(values):
    high = lax.reduce_precision(values, exponent_bits=8, mantissa_bits=7)
    return high.astype(jnp.bfloat16), (values - high).astype(jnp.bfloat16)


def split_here(values):
    high = values.astype(jnp.bfloat16)
    return high, (values - high.astype(jnp.float32)).astype(jnp.bfloat16)


def triple_dot(left_high, left_low, right_high, right_low):
    left = jnp.concatenate([left_high, left_high, left_low], 1)
    right = jnp.concatenate([right_high, right_low, right_high], 0)
    return jnp.dot(left, right, preferred_element_type=jnp.float32)


def params(limit):
    return pltpu.CompilerParams(vmem_limit_bytes=limit * MIB)


def cost(flops, bytes_accessed):
    return pl.CostEstimate(flops=flops, bytes_accessed=bytes_accessed, transcendentals=0)


def exchange(value, axis, size, step):
    return lax.ppermute(value, axis, [(i, i ^ step) for i in range(size)])


def mask_kernel(panel_ref, mask_ref, token_ref, out_ref):
    out_ref[...] = panel_ref[0] * mask_ref[0]


def masked(panels, mask, token, j, lo, hi):
    rows = panels.shape[2]
    count = hi - lo
    return pl.pallas_call(
        mask_kernel,
        grid=(1,),
        out_shape=jax.ShapeDtypeStruct((count, rows), jnp.float32),
        in_specs=[
            pl.BlockSpec((1, count, rows), lambda i: (j, lo // count, 0)),
            pl.BlockSpec((1, 1, rows), lambda i: (j, 0, 0)),
            pl.BlockSpec(memory_space=pl.ANY),
        ],
        out_specs=pl.BlockSpec((count, rows), lambda i: (0, 0)),
        compiler_params=params(32),
        cost_estimate=cost(count * rows, 8 * count * rows),
        name="masked",
    )(panels, mask, token)


def prepare_kernel(order_ref, a_ref, token_ref, high_ref, low_ref):
    high_ref[0], low_ref[0] = split_here(a_ref[...])


def prepared(ainv, order, token, count, part):
    rows = ainv.shape[0]
    if part % 128:
        pieces = [
            split(lax.dynamic_slice_in_dim(ainv, order[s] * part, part, 1)) for s in range(count)
        ]
        return jnp.stack([p[0] for p in pieces], 0), jnp.stack([p[1] for p in pieces], 0)
    tile = tile_of(rows, 1024)
    shape = jax.ShapeDtypeStruct((count, rows, part), jnp.bfloat16)
    spec = pl.BlockSpec((1, tile, part), lambda s, i, order: (s, i, 0))
    return pl.pallas_call(
        prepare_kernel,
        out_shape=(shape, shape),
        grid_spec=pltpu.PrefetchScalarGridSpec(
            num_scalar_prefetch=1,
            grid=(count, rows // tile),
            in_specs=[
                pl.BlockSpec((tile, part), lambda s, i, order: (i, order[s])),
                pl.BlockSpec(memory_space=pl.ANY),
            ],
            out_specs=(spec, spec),
        ),
        compiler_params=params(32),
        cost_estimate=cost(4 * ainv.size, 8 * ainv.size),
        name="prepared",
    )(order, ainv, token)


def product_kernel(first, count, depth, with_pre, with_split, *refs):
    refs = list(refs)
    if with_split:
        gathered_ref = refs.pop(0)
        pre_ref = refs.pop(0) if with_pre else None
        a_high_ref, a_low_ref = refs.pop(0), refs.pop(0)
        high_ref, low_ref = refs.pop(0), refs.pop(0)
    else:
        high_ref, low_ref = refs.pop(0), refs.pop(0)
        a_high_ref, a_low_ref = refs.pop(0), refs.pop(0)
    outs, total_ref = refs[:count], refs[count]
    s, n = pl.program_id(0), pl.program_id(1)
    rows = high_ref.shape[0]

    if with_split:
        strip = 16

        @pl.when((s == 0) & (n == 0))
        def _():
            @pl.loop(0, rows // strip)
            def _(i):
                here = pl.ds(pl.multiple_of(i * strip, strip), strip)
                values = gathered_ref[here, :]
                if with_pre:
                    values = values - pre_ref[here, :]
                high_ref[here, :], low_ref[here, :] = split_here(values)

    steps = high_ref.shape[1] // depth

    @pl.loop(0, steps)
    def _(k):
        here = pl.ds(pl.multiple_of(k * depth, depth), depth)
        value = triple_dot(
            high_ref[:, here], low_ref[:, here], a_high_ref[0, here, :], a_low_ref[0, here, :]
        )

        @pl.when(k == 0)
        def _():
            total_ref[...] = value

        @pl.when(k > 0)
        def _():
            total_ref[...] += value

    for i in range(count):
        @pl.when(s == i)
        def _():
            outs[i][...] = total_ref[...]


def products(factor, inverse, first, last, pre=None):
    with_split = not isinstance(factor, tuple)
    a_high, a_low = inverse
    count = last - first
    part = a_high.shape[2]
    rows, depth_all = (factor if with_split else factor[0]).shape
    tile = tile_of(part, 256)
    tiles = part // tile
    once = pl.Buffered(1)
    whole = pl.BlockSpec((rows, depth_all), lambda s, n: (0, 0), pipeline_mode=once)
    a_spec = pl.BlockSpec((1, depth_all, tile), lambda s, n: (s + first, 0, n))

    def out_spec(i):
        return pl.BlockSpec(
            (rows, tile), lambda s, n: (0, jnp.where(s < i, 0, jnp.where(s > i, tiles - 1, n)))
        )

    out_shape = [jax.ShapeDtypeStruct((rows, part), jnp.float32)] * count
    out_specs = [out_spec(i) for i in range(count)]
    if with_split:
        operands = [factor] + ([] if pre is None else [pre]) + [a_high, a_low]
        in_specs = [whole] * (len(operands) - 2) + [a_spec, a_spec]
        out_shape = [jax.ShapeDtypeStruct((rows, depth_all), jnp.bfloat16)] * 2 + out_shape
        out_specs = [pl.BlockSpec((rows, depth_all), lambda s, n: (0, 0))] * 2 + out_specs
    else:
        operands = [factor[0], factor[1], a_high, a_low]
        in_specs = [whole, whole, a_spec, a_spec]
    got = pl.pallas_call(
        functools.partial(
            product_kernel, first, count, tile_of(depth_all, 1024), pre is not None, with_split
        ),
        grid=(count, tiles),
        out_shape=out_shape,
        in_specs=in_specs,
        out_specs=out_specs,
        scratch_shapes=[pltpu.VMEM((rows, tile), jnp.float32)],
        compiler_params=params(56),
        cost_estimate=cost(
            6 * rows * depth_all * part * count, 4 * depth_all * part * count + 8 * rows * depth_all
        ),
        name="products",
    )(*operands)
    if with_split:
        return (got[0], got[1]), list(got[2:])
    return factor, list(got)


def elimination_kernel(count, *refs):
    value = None
    for i in range(count):
        c_high, c_low, f_high, f_low = (r[...] for r in refs[4 * i : 4 * i + 4])
        term = triple_dot(c_high, c_low, f_high, f_low)
        value = term if value is None else value + term
    refs[-1][...] = value


def elimination(pairs):
    operands = []
    for coupled, (high, low) in pairs:
        operands += [*split(coupled), high, low]
    rows, depth = pairs[0][0].shape
    length = pairs[0][1][0].shape[1]
    tile = tile_of(length, 512)
    left = pl.BlockSpec((rows, depth), lambda i: (0, 0))
    right = pl.BlockSpec((depth, tile), lambda i: (0, i))
    return pl.pallas_call(
        functools.partial(elimination_kernel, len(pairs)),
        grid=(length // tile,),
        out_shape=jax.ShapeDtypeStruct((rows, length), jnp.float32),
        in_specs=[left, left, right, right] * len(pairs),
        out_specs=pl.BlockSpec((rows, tile), lambda i: (0, i)),
        compiler_params=params(48),
        cost_estimate=cost(
            6 * rows * depth * length * len(pairs), 4 * length * (rows + depth * len(pairs))
        ),
        name="elimination",
    )(*operands)


def inner_products(left, right):
    nt = (((1,), (1,)), ((), ()))
    high, low = split(left)
    rows = left.shape[0]
    both = lax.dot_general(
        jnp.concatenate([high, low], 0), right[0], nt, preferred_element_type=jnp.float32
    )
    cross = lax.dot_general(high, right[1], nt, preferred_element_type=jnp.float32)
    return both[:rows] + both[rows:] + cross


def shards(ainv, panels, pattern, coupling, dinv):
    rows_n = lax.axis_size("prow")
    cols_n = lax.axis_size("pcol")
    row = lax.axis_index("prow")
    col = lax.axis_index("pcol")
    local_rows, local_cols = panels.shape[1:]
    part = ainv.shape[1] // rows_n
    ratio = cols_n // rows_n
    blocks_here = local_rows // NB

    flags = lax.dynamic_slice_in_dim(pattern, row * blocks_here, blocks_here, 1)
    mask = jnp.repeat(flags.astype(jnp.float32), NB, axis=1)[:, None, :]
    turned = jnp.swapaxes(panels, 1, 2)

    cut = local_cols * 3 // 4
    chunks = [(0, 0, local_cols), (1, 0, local_cols), (2, 0, cut), (2, cut, local_cols)]

    order = row ^ jnp.arange(rows_n, dtype=jnp.int32)
    gathered = []
    for i, (j, lo, hi) in enumerate(chunks):
        token = gathered[i - 1] if i else mask
        shard = masked(turned, mask, token, j, lo, hi)
        if i == 0:
            inverse = prepared(ainv, order, shard, rows_n, part)
        gathered.append(lax.all_gather(shard, "pcol", axis=0, tiled=True))

    def columns(matrix, lo, hi):
        whole = matrix.shape[0]
        kept = matrix.reshape(whole, cols_n, local_cols)[:, :, lo:hi].reshape(whole, -1)
        return kept.T

    factors = []
    finished = []
    for (j, lo, hi), value in zip(chunks, gathered):
        pre = None
        if j == 1:
            pre = elimination([(columns(coupling[0], lo, hi), factors[0])])
        if j == 2:
            pre = elimination(
                [
                    (columns(coupling[1], lo, hi), factors[0]),
                    (columns(coupling[2], lo, hi), factors[1]),
                ]
            )
        factor, sent = products(value, inverse, 1, rows_n, pre)
        factors.append(factor)
        received = [exchange(sent[s - 1], "prow", rows_n, s) for s in range(1, rows_n)]
        _, (total,) = products(factor, inverse, 0, 1)
        for other in received:
            total = total + other
        count = hi - lo
        moved = lax.all_to_all((-total).reshape(cols_n, count, part), "pcol", 0, 0)
        moved = lax.all_to_all(moved.reshape(rows_n, ratio * count, part), "prow", 0, 0)
        moved = moved.reshape(rows_n, ratio, count, part).transpose(2, 1, 0, 3)
        finished.append(moved.reshape(count, local_rows))

    groups = [
        [(0, 0), (0, 1), (1, 1)],
        [(0, 2), (1, 2), (2, 2)],
        [(0, 3), (1, 3), (2, 3)],
        [(3, 2), (3, 3)],
    ]
    inner = {}
    for group in groups:
        terms = [inner_products(-finished[a], factors[b]) for a, b in group]
        flat = [t.reshape(-1, 128) for t in terms]
        joined = jnp.concatenate(flat, 0)
        summed = joined
        for s in range(1, rows_n):
            summed = summed + exchange(joined, "prow", rows_n, s)
        for (a, b), t, f in zip(group, terms, flat):
            inner[a, b] = summed[: f.shape[0]].reshape(t.shape)
            summed = summed[f.shape[0] :]

    def block(j, k):
        strips = []
        for a, (ja, lo, hi) in enumerate(chunks):
            if ja != j:
                continue
            pieces = [
                inner[a, b].reshape(hi - lo, cols_n, -1)
                for b, (kb, _, _) in enumerate(chunks)
                if kb == k
            ]
            strips.append(jnp.concatenate(pieces, 2).reshape(hi - lo, cols_n * local_cols))
        return jnp.concatenate(strips, 0)

    inner = [[block(j, k) for k in range(j, 3)] for j in range(3)]

    first, second, third = coupling[0], coupling[1], coupling[2]
    start = col * local_cols

    def own_rows(matrix):
        return lax.dynamic_slice_in_dim(matrix, start, local_cols, 0)

    def own_cols(matrix):
        return lax.dynamic_slice_in_dim(matrix, start, local_cols, 1)

    bridge = second - matmul(first, third)
    d0 = own_rows(dinv[0])
    d1 = own_rows(dinv[1])
    k0 = tdot(own_cols(first), dinv[0])
    k1 = tdot(own_cols(bridge), dinv[0])
    k2 = tdot(own_cols(third), dinv[1])
    diag_zero = d0 + inner[0][0]
    cross_one = inner[0][1] - matmul(d0, first)
    cross_two = inner[0][2] - matmul(d0, bridge)
    diag_one = inner[1][0] + (d1 + matmul(k0, first))
    cross_three = inner[1][1] + (matmul(k0, bridge) - matmul(d1, third))
    diag_two = inner[2][0] + (own_rows(dinv[2]) + matmul(k1, bridge) + matmul(k2, third))

    panel_parts = [[], [], []]
    for (j, lo, hi), value in zip(chunks, finished):
        panel_parts[j].append(value)
    xpanel = jnp.stack([jnp.concatenate(p, 0) for p in panel_parts], 0)
    xcross = jnp.stack([cross_one, cross_two, cross_three], 0)
    ydiag = jnp.stack([diag_zero, diag_one, diag_two], 0)
    return (jnp.swapaxes(xpanel, 1, 2), xcross, ydiag)


def solution(mesh):
    placed = (P("prow", "pcol"), P(None, "prow", "pcol"), P(), P(), P())
    return jax.shard_map(
        shards,
        mesh=mesh,
        in_specs=placed,
        out_specs=(P(None, "prow", "pcol"), P(None, "pcol", None), P(None, "pcol", None)),
        check_vma=False,
    )
```

```python
import functools

import jax
import jax.numpy as jnp
from jax import lax
from jax.experimental import pallas as pl
from jax.experimental.pallas import tpu as pltpu
from jax.sharding import PartitionSpec as P

NB = 128
MIB = 1024 * 1024

precise = lax.Precision.HIGHEST


def matmul(left, right):
    return jnp.dot(left, right, precision=precise, preferred_element_type=jnp.float32)


def tdot(left, right):
    return lax.dot_general(
        left, right, (((0,), (0,)), ((), ())), precision=precise, preferred_element_type=jnp.float32
    )


def tile_of(size, wanted):
    return wanted if size % wanted == 0 else size


def split(values):
    high = lax.reduce_precision(values, exponent_bits=8, mantissa_bits=7)
    return high.astype(jnp.bfloat16), (values - high).astype(jnp.bfloat16)


def split_here(values):
    high = values.astype(jnp.bfloat16)
    return high, (values - high.astype(jnp.float32)).astype(jnp.bfloat16)


def triple_dot(left_high, left_low, right_high, right_low):
    left = jnp.concatenate([left_high, left_high, left_low], 1)
    right = jnp.concatenate([right_high, right_low, right_high], 0)
    return jnp.dot(left, right, preferred_element_type=jnp.float32)


def exchange(value, axis, size, step):
    return lax.ppermute(value, axis, [(i, i ^ step) for i in range(size)])


class Order:
    def __init__(self):
        self.last = None

    def __call__(self, kernel, operands, in_specs, out_shape, out_specs, grid, flops, moved,
                 name, scratch=(), limit=56, prefetch=(), extra=()):
        tokens = list(extra) + ([] if self.last is None else [self.last])
        skip = len(prefetch) + len(operands)

        def body(*refs):
            kernel(*refs[:skip], *refs[skip + len(tokens):])

        got = pl.pallas_call(
            body,
            out_shape=out_shape,
            grid_spec=pltpu.PrefetchScalarGridSpec(
                num_scalar_prefetch=len(prefetch),
                grid=grid,
                in_specs=list(in_specs) + [pl.BlockSpec(memory_space=pl.ANY)] * len(tokens),
                out_specs=out_specs,
                scratch_shapes=list(scratch),
            ),
            compiler_params=pltpu.CompilerParams(vmem_limit_bytes=limit * MIB),
            cost_estimate=pl.CostEstimate(flops=flops, bytes_accessed=moved, transcendentals=0),
            name=name,
        )(*prefetch, *operands, *tokens)
        self.last = got[0] if isinstance(got, (tuple, list)) else got
        return got


def shape_of(shape, dtype=jnp.float32):
    return jax.ShapeDtypeStruct(shape, dtype)


def mask_kernel(panel_ref, mask_ref, out_ref):
    out_ref[...] = panel_ref[0] * mask_ref[0]


def masked(order, panels, mask, j, lo, hi, extra):
    rows = panels.shape[2]
    count = hi - lo
    return order(
        mask_kernel,
        [panels, mask],
        [
            pl.BlockSpec((1, count, rows), lambda i: (j, lo // count, 0)),
            pl.BlockSpec((1, 1, rows), lambda i: (j, 0, 0)),
        ],
        shape_of((count, rows)),
        pl.BlockSpec((count, rows), lambda i: (0, 0)),
        (1,),
        count * rows,
        8 * count * rows,
        "masked",
        extra=extra,
    )


def prepare_kernel(partner_ref, a_ref, high_ref, low_ref):
    high_ref[0], low_ref[0] = split_here(a_ref[...])


def prepared(order, ainv, partner, count, part):
    rows = ainv.shape[0]
    if part % 128:
        pieces = [
            split(lax.dynamic_slice_in_dim(ainv, partner[s] * part, part, 1)) for s in range(count)
        ]
        return jnp.stack([p[0] for p in pieces], 0), jnp.stack([p[1] for p in pieces], 0)
    tile = tile_of(rows, 1024)
    shape = shape_of((count, rows, part), jnp.bfloat16)
    spec = pl.BlockSpec((1, tile, part), lambda s, i, partner: (s, i, 0))
    return order(
        prepare_kernel,
        [ainv],
        [pl.BlockSpec((tile, part), lambda s, i, partner: (i, partner[s]))],
        (shape, shape),
        (spec, spec),
        (count, rows // tile),
        4 * ainv.size,
        8 * ainv.size,
        "prepared",
        prefetch=[partner],
    )


def product_kernel(count, steps, with_pre, with_split, *refs):
    refs = list(refs)
    s, k = pl.program_id(0), pl.program_id(1)
    if with_split:
        gathered_ref = refs.pop(0)
        pre_ref = refs.pop(0) if with_pre else None
        a_high_ref, a_low_ref = refs.pop(0), refs.pop(0)
        high_ref, low_ref = refs.pop(0), refs.pop(0)
        rows, depth = gathered_ref.shape
        here = pl.ds(pl.multiple_of(k * depth, depth), depth)

        @pl.when(s == 0)
        def _():
            strip = 16

            @pl.loop(0, rows // strip)
            def _(i):
                rows_here = pl.ds(pl.multiple_of(i * strip, strip), strip)
                values = gathered_ref[rows_here, :]
                if with_pre:
                    values = values - pre_ref[rows_here, :]
                high_ref[rows_here, here], low_ref[rows_here, here] = split_here(values)

        high, low = high_ref[:, here], low_ref[:, here]
    else:
        high_ref, low_ref, a_high_ref, a_low_ref = refs[:4]
        refs = refs[4:]
        high, low = high_ref[...], low_ref[...]
    outs, total_ref = refs[:count], refs[count]
    value = triple_dot(high, low, a_high_ref[0], a_low_ref[0])

    @pl.when(k == 0)
    def _():
        total_ref[...] = value

    @pl.when(k > 0)
    def _():
        total_ref[...] += value

    for i in range(count):
        @pl.when((s == i) & (k == steps - 1))
        def _():
            outs[i][...] = total_ref[...]


def products(order, factor, inverse, first, last, pre=None):
    with_split = not isinstance(factor, tuple)
    a_high, a_low = inverse
    count = last - first
    part = a_high.shape[2]
    rows, length = (factor if with_split else factor[0]).shape
    depth = tile_of(length, 1024)
    steps = length // depth
    a_spec = pl.BlockSpec((1, depth, part), lambda s, k: (s + first, k, 0))
    out_shape = [shape_of((rows, part))] * count
    out_specs = [pl.BlockSpec((rows, part), lambda s, k: (0, 0))] * count
    if with_split:
        operands = [factor] + ([] if pre is None else [pre]) + [a_high, a_low]
        once = pl.BlockSpec((rows, depth), lambda s, k: (0, jnp.where(s == 0, k, steps - 1)))
        in_specs = [once] * (len(operands) - 2) + [a_spec, a_spec]
        out_shape = [shape_of((rows, length), jnp.bfloat16)] * 2 + out_shape
        out_specs = [pl.BlockSpec((rows, length), lambda s, k: (0, 0))] * 2 + out_specs
    else:
        operands = [factor[0], factor[1], a_high, a_low]
        in_specs = [pl.BlockSpec((rows, depth), lambda s, k: (0, k))] * 2 + [a_spec, a_spec]
    got = order(
        functools.partial(product_kernel, count, steps, pre is not None, with_split),
        operands,
        in_specs,
        out_shape,
        out_specs,
        (count, steps),
        6 * rows * length * part * count,
        4 * length * part * count + 8 * rows * length,
        "products",
        scratch=[pltpu.VMEM((rows, part), jnp.float32)],
    )
    if with_split:
        return (got[0], got[1]), list(got[2:])
    return factor, list(got)


def elimination_kernel(sources, sizes, *refs):
    value = None
    for i in range(sources):
        c_high, c_low, f_high, f_low = (r[...] for r in refs[4 * i : 4 * i + 4])
        term = triple_dot(c_high, c_low, f_high, f_low)
        value = term if value is None else value + term
    start = 0
    for ref, size in zip(refs[4 * sources :], sizes):
        ref[...] = value[start : start + size]
        start += size


def elimination(order, pairs, sizes):
    operands = []
    for coupled, factor in pairs:
        operands += [*coupled, *factor]
    rows, depth = pairs[0][0][0].shape
    length = pairs[0][1][0].shape[1]
    tile = tile_of(length, 512)
    left = pl.BlockSpec((rows, depth), lambda i: (0, 0))
    right = pl.BlockSpec((depth, tile), lambda i: (0, i))
    return order(
        functools.partial(elimination_kernel, len(pairs), sizes),
        operands,
        [left, left, right, right] * len(pairs),
        [shape_of((size, length)) for size in sizes],
        [pl.BlockSpec((size, tile), lambda i: (0, i)) for size in sizes],
        (length // tile,),
        6 * rows * depth * length * len(pairs),
        4 * length * (rows + depth * len(pairs)),
        "elimination",
    )


def sum_kernel(sign, *refs):
    value = refs[0][...]
    for ref in refs[1:-1]:
        value = value + ref[...]
    refs[-1][...] = sign * value


def signed_sum(order, sign, terms):
    rows, width = terms[0].shape
    tile = tile_of(rows, 128)
    spec = pl.BlockSpec((tile, width), lambda i: (i, 0))
    size = rows * width
    return order(
        functools.partial(sum_kernel, sign), terms, [spec] * len(terms), shape_of((rows, width)), spec, (rows // tile,),
        len(terms) * size, 4 * (len(terms) + 1) * size, "signed_sum",
    )


def relay_kernel(in_ref, out_ref):
    out_ref[...] = in_ref[...]


def relay(order, value):
    block = (value.shape[0] // 2, *value.shape[1:])
    spec = pl.BlockSpec(block, lambda i: (i, 0, 0))
    return order(
        relay_kernel, [value], [spec], shape_of(value.shape), spec, (2,),
        value.size, 8 * value.size, "relay",
    )


def assembly_kernel(in_ref, out_ref):
    outer, inner, _, part = in_ref.shape
    for a in range(inner):
        for q in range(outer):
            out_ref[:, pl.ds((a * outer + q) * part, part)] = in_ref[q, a]


def assembled(order, value):
    outer, inner, count, part = value.shape
    shape = (count, outer * inner * part)
    return order(
        assembly_kernel,
        [value],
        [pl.BlockSpec(value.shape, lambda i: (0, 0, 0, 0))],
        shape_of(shape),
        pl.BlockSpec(shape, lambda i: (0, 0)),
        (1,),
        value.size,
        8 * value.size,
        "assembled",
    )


def inner_kernel(lefts_n, rights_n, terms, *refs):
    lefts = [r[...] for r in refs[:lefts_n]]
    rights = refs[lefts_n : lefts_n + 2 * rights_n]
    outs = refs[lefts_n + 2 * rights_n :]
    nt = (((1,), (1,)), ((), ()))

    @pl.when(pl.program_id(0) == 0)
    def _():
        for out in outs:
            out[...] = jnp.zeros_like(out)

    for (which, right), out in zip(terms, outs):
        left = jnp.concatenate([lefts[a] for a in which], 0) if len(which) > 1 else lefts[which[0]]
        high, low = split_here(-left)
        r_high, r_low = rights[2 * right][...], rights[2 * right + 1][...]
        triple = jnp.concatenate([high, low, high], 1)
        other = jnp.concatenate([r_high, r_high, r_low], 1)
        out[...] += lax.dot_general(triple, other, nt, preferred_element_type=jnp.float32)


def inner_products(order, lefts, rights, terms):
    length = lefts[0].shape[1]
    depth = tile_of(length, 1024)
    shapes = [
        (sum(lefts[a].shape[0] for a in which), rights[right][0].shape[0]) for which, right in terms
    ]
    flat = [part for right in rights for part in right]
    return order(
        functools.partial(inner_kernel, len(lefts), len(rights), terms),
        list(lefts) + flat,
        [pl.BlockSpec((v.shape[0], depth), lambda k: (0, k)) for v in list(lefts) + flat],
        [shape_of(s) for s in shapes],
        [pl.BlockSpec(s, lambda k: (0, 0)) for s in shapes],
        (length // depth,),
        sum(6 * a * b * length for a, b in shapes),
        sum(2 * v.size for v in flat) + sum(4 * v.size for v in lefts),
        "inner_products",
    )


def shards(ainv, panels, pattern, coupling, dinv):
    rows_n = lax.axis_size("prow")
    cols_n = lax.axis_size("pcol")
    row = lax.axis_index("prow")
    col = lax.axis_index("pcol")
    local_rows, local_cols = panels.shape[1:]
    part = ainv.shape[1] // rows_n
    ratio = cols_n // rows_n
    blocks_here = local_rows // NB

    flags = lax.dynamic_slice_in_dim(pattern, row * blocks_here, blocks_here, 1)
    mask = jnp.repeat(flags.astype(jnp.float32), NB, axis=1)[:, None, :]
    turned = jnp.swapaxes(panels, 1, 2)

    cut = local_cols * 3 // 4
    chunks = [(0, 0, local_cols), (1, 0, local_cols), (2, 0, cut), (2, cut, local_cols)]
    last_cuts = [(0, cut), (cut, local_cols)]
    partner = row ^ jnp.arange(rows_n, dtype=jnp.int32)

    def columns(matrix, cuts):
        cube = matrix.reshape(matrix.shape[0], cols_n, local_cols)
        kept = [cube[:, :, lo:hi].reshape(matrix.shape[0], -1) for lo, hi in cuts]
        return split(jnp.concatenate(kept, 1).T)

    c_one = columns(coupling[0], [(0, local_cols)])
    c_two = columns(coupling[1], last_cuts)
    c_three = columns(coupling[2], last_cuts)

    def gather(shard):
        return lax.all_gather(shard, "pcol", axis=0, tiled=True)

    def send(pieces):
        return [exchange(p, "prow", rows_n, s + 1) for s, p in enumerate(pieces)]

    def to_columns(total):
        count = total.shape[0] // cols_n
        return lax.all_to_all(total.reshape(cols_n, count, part), "pcol", 0, 0)

    def to_rows(value):
        count = value.shape[1]
        value = value.reshape(rows_n, ratio * count, part)
        value = lax.all_to_all(value, "prow", 0, 0)
        return value.reshape(rows_n, ratio, count, part)

    def share(terms):
        flat = jnp.concatenate([t.reshape(-1, 128) for t in terms], 0)
        received = [exchange(flat, "prow", rows_n, s) for s in range(1, rows_n)]
        return [t.shape for t in terms], [flat] + received

    def add_up(sent):
        shapes, parts = sent
        total = signed_sum(order, 1.0, parts)
        out = []
        for shape in shapes:
            size = shape[0] * shape[1] // 128
            out.append(total[:size].reshape(shape))
            total = total[size:]
        return out

    order = Order()
    shard = masked(order, turned, mask, *chunks[0], [])
    g0 = gather(shard)
    inverse = prepared(order, ainv, partner, rows_n, part)

    shard = masked(order, turned, mask, *chunks[1], [g0, c_one[0], c_two[0], c_three[0]])
    g1 = gather(shard)
    f0, sent = products(order, g0, inverse, 1, rows_n)
    r0 = send(sent)
    _, own0 = products(order, f0, inverse, 0, 1)
    pre1 = elimination(order, [(c_one, f0)], [cols_n * local_cols])

    shard = masked(order, turned, mask, *chunks[2], [g1])
    g2 = gather(shard)
    f1, sent = products(order, g1, inverse, 1, rows_n, pre1[0])
    r1 = send(sent)
    m0 = to_columns(signed_sum(order, -1.0, own0 + r0))
    _, own1 = products(order, f1, inverse, 0, 1)
    pre2 = elimination(
        order, [(c_two, f0), (c_three, f1)], [cols_n * (hi - lo) for lo, hi in last_cuts]
    )

    shard = masked(order, turned, mask, *chunks[3], [g2])
    g3 = gather(shard)
    f2, sent = products(order, g2, inverse, 1, rows_n, pre2[0])
    r2 = send(sent)
    m0 = to_rows(relay(order, m0))
    m1 = to_columns(signed_sum(order, -1.0, own1 + r1))
    _, own2 = products(order, f2, inverse, 0, 1)

    f3, sent = products(order, g3, inverse, 1, rows_n, pre2[1])
    r3 = send(sent)
    m2 = to_columns(signed_sum(order, -1.0, own2 + r2))
    _, own3 = products(order, f3, inverse, 0, 1)
    m1 = to_rows(relay(order, m1))
    x0 = assembled(order, m0)
    m3 = to_columns(signed_sum(order, -1.0, own3 + r3))
    m2 = to_rows(relay(order, m2))
    x1 = assembled(order, m1)
    early = inner_products(order, [x0, x1], [f0, f1], (((0,), 0), ((0, 1), 1)))
    early = share(early)
    m3 = to_rows(relay(order, m3))
    x2 = assembled(order, m2)
    late = inner_products(order, [x0, x1, x2], [f2, f3], (((0, 1, 2), 0), ((0, 1, 2), 1)))
    late = share(late)
    early = add_up(early)
    x3 = assembled(order, m3)
    final = inner_products(order, [x3], [f2, f3], (((0,), 0), ((0,), 1)))
    final = share(final)
    late = add_up(late)
    final = add_up(final)

    def join(parts):
        cubes = [p.reshape(p.shape[0], cols_n, -1) for p in parts]
        return jnp.concatenate(cubes, 2).reshape(parts[0].shape[0], cols_n * local_cols)

    late = join(late)
    two = local_cols * 2
    inner = [
        [early[0], early[1][:local_cols], late[:local_cols]],
        [early[1][local_cols:], late[local_cols:two]],
        [jnp.concatenate([late[two:], join(final)], 0)],
    ]
    finished = [x0, x1, x2, x3]

    first, second, third = coupling[0], coupling[1], coupling[2]
    start = col * local_cols

    def own_rows(matrix):
        return lax.dynamic_slice_in_dim(matrix, start, local_cols, 0)

    def own_cols(matrix):
        return lax.dynamic_slice_in_dim(matrix, start, local_cols, 1)

    bridge = second - matmul(first, third)
    d0 = own_rows(dinv[0])
    d1 = own_rows(dinv[1])
    k0 = tdot(own_cols(first), dinv[0])
    k1 = tdot(own_cols(bridge), dinv[0])
    k2 = tdot(own_cols(third), dinv[1])
    diag_zero = d0 + inner[0][0]
    cross_one = inner[0][1] - matmul(d0, first)
    cross_two = inner[0][2] - matmul(d0, bridge)
    diag_one = inner[1][0] + (d1 + matmul(k0, first))
    cross_three = inner[1][1] + (matmul(k0, bridge) - matmul(d1, third))
    diag_two = inner[2][0] + (own_rows(dinv[2]) + matmul(k1, bridge) + matmul(k2, third))

    panel_parts = [[], [], []]
    for (j, lo, hi), value in zip(chunks, finished):
        panel_parts[j].append(value)
    xpanel = jnp.stack([jnp.concatenate(p, 0) for p in panel_parts], 0)
    xcross = jnp.stack([cross_one, cross_two, cross_three], 0)
    ydiag = jnp.stack([diag_zero, diag_one, diag_two], 0)
    return (jnp.swapaxes(xpanel, 1, 2), xcross, ydiag)


def solution(mesh):
    placed = (P("prow", "pcol"), P(None, "prow", "pcol"), P(), P(), P())
    return jax.shard_map(
        shards,
        mesh=mesh,
        in_specs=placed,
        out_specs=(P(None, "prow", "pcol"), P(None, "pcol", None), P(None, "pcol", None)),
        check_vma=False,
    )
```

```python
import functools

import jax
import jax.numpy as jnp
from jax import lax
from jax.experimental import pallas as pl
from jax.experimental.pallas import tpu as pltpu
from jax.sharding import PartitionSpec as P

NB = 128
MIB = 1024 * 1024

precise = lax.Precision.HIGHEST


def matmul(left, right):
    return jnp.dot(left, right, precision=precise, preferred_element_type=jnp.float32)


def tdot(left, right):
    return lax.dot_general(
        left, right, (((0,), (0,)), ((), ())), precision=precise, preferred_element_type=jnp.float32
    )


def tile_of(size, wanted):
    return wanted if size % wanted == 0 else size


def split(values):
    high = lax.reduce_precision(values, exponent_bits=8, mantissa_bits=7)
    return high.astype(jnp.bfloat16), (values - high).astype(jnp.bfloat16)


def split_here(values):
    high = values.astype(jnp.bfloat16)
    return high, (values - high.astype(jnp.float32)).astype(jnp.bfloat16)


def triple_dot(left_high, left_low, right_high, right_low, contract=(1, 0)):
    dims = (((contract[0],), (contract[1],)), ((), ()))

    def dot(left, right):
        return lax.dot_general(left, right, dims, preferred_element_type=jnp.float32)

    return dot(left_high, right_high) + dot(left_high, right_low) + dot(left_low, right_high)


def exchange(value, axis, size, step):
    return lax.ppermute(value, axis, [(i, i ^ step) for i in range(size)])


class Order:
    def __init__(self):
        self.last = None

    def __call__(self, kernel, operands, in_specs, out_shape, out_specs, grid, flops, moved,
                 name, scratch=(), limit=56, prefetch=(), extra=(), aliases=None):
        tokens = list(extra) + ([] if self.last is None else [self.last])
        skip = len(prefetch) + len(operands)

        def body(*refs):
            kernel(*refs[:skip], *refs[skip + len(tokens):])

        got = pl.pallas_call(
            body,
            out_shape=out_shape,
            grid_spec=pltpu.PrefetchScalarGridSpec(
                num_scalar_prefetch=len(prefetch),
                grid=grid,
                in_specs=list(in_specs) + [pl.BlockSpec(memory_space=pl.ANY)] * len(tokens),
                out_specs=out_specs,
                scratch_shapes=list(scratch),
            ),
            compiler_params=pltpu.CompilerParams(vmem_limit_bytes=limit * MIB),
            cost_estimate=pl.CostEstimate(
                flops=flops // 16, bytes_accessed=moved // 16, transcendentals=0
            ),
            input_output_aliases=aliases or {},
            name=name,
        )(*prefetch, *operands, *tokens)
        self.last = got[0] if isinstance(got, (tuple, list)) else got
        return got


def shape_of(shape, dtype=jnp.float32):
    return jax.ShapeDtypeStruct(shape, dtype)


def mask_kernel(panel_ref, mask_ref, out_ref):
    out_ref[...] = panel_ref[0] * mask_ref[0]


def masked(order, panels, mask, j, lo, hi, extra):
    rows = panels.shape[2]
    count = hi - lo
    return order(
        mask_kernel,
        [panels, mask],
        [
            pl.BlockSpec((1, count, rows), lambda i: (j, lo // count, 0)),
            pl.BlockSpec((1, 1, rows), lambda i: (j, 0, 0)),
        ],
        shape_of((count, rows)),
        pl.BlockSpec((count, rows), lambda i: (0, 0)),
        (1,),
        count * rows,
        8 * count * rows,
        "masked",
        extra=extra,
    )


def prepare_kernel(partner_ref, a_ref, high_ref, low_ref):
    high_ref[0], low_ref[0] = split_here(a_ref[...])


def prepared(order, ainv, partner, count, part):
    rows = ainv.shape[0]
    if part % 128:
        pieces = [
            split(lax.dynamic_slice_in_dim(ainv, partner[s] * part, part, 1)) for s in range(count)
        ]
        return jnp.stack([p[0] for p in pieces], 0), jnp.stack([p[1] for p in pieces], 0)
    tile = tile_of(rows, 1024)
    shape = shape_of((count, rows, part), jnp.bfloat16)
    spec = pl.BlockSpec((1, tile, part), lambda s, i, partner: (s, i, 0))
    return order(
        prepare_kernel,
        [ainv],
        [pl.BlockSpec((tile, part), lambda s, i, partner: (i, partner[s]))],
        (shape, shape),
        (spec, spec),
        (count, rows // tile),
        4 * ainv.size,
        8 * ainv.size,
        "prepared",
        prefetch=[partner],
    )


def product_kernel(count, steps, with_pre, with_split, *refs):
    refs = list(refs)
    s, k = pl.program_id(0), pl.program_id(1)
    if with_split:
        gathered_ref = refs.pop(0)
        pre_ref = refs.pop(0) if with_pre else None
        a_high_ref, a_low_ref = refs.pop(0), refs.pop(0)
        high_ref, low_ref = refs.pop(0), refs.pop(0)
        rows, depth = gathered_ref.shape
        here = pl.ds(pl.multiple_of(k * depth, depth), depth)

        @pl.when(s == 0)
        def _():
            strip = 16

            @pl.loop(0, rows // strip)
            def _(i):
                rows_here = pl.ds(pl.multiple_of(i * strip, strip), strip)
                values = gathered_ref[rows_here, :]
                if with_pre:
                    values = values - pre_ref[rows_here, :]
                high_ref[rows_here, here], low_ref[rows_here, here] = split_here(values)

        high, low = high_ref[:, here], low_ref[:, here]
    else:
        high_ref, low_ref, a_high_ref, a_low_ref = refs[:4]
        refs = refs[4:]
        high, low = high_ref[...], low_ref[...]
    outs, total_ref = refs[:count], refs[count]
    value = triple_dot(high, low, a_high_ref[0], a_low_ref[0])

    @pl.when(k == 0)
    def _():
        total_ref[...] = value

    @pl.when(k > 0)
    def _():
        total_ref[...] += value

    for i in range(count):
        @pl.when((s == i) & (k == steps - 1))
        def _():
            outs[i][...] = total_ref[...]


def products(order, factor, inverse, first, last, pre=None):
    with_split = not isinstance(factor, tuple)
    a_high, a_low = inverse
    count = last - first
    part = a_high.shape[2]
    rows, length = (factor if with_split else factor[0]).shape
    depth = tile_of(length, 1024)
    steps = length // depth
    a_spec = pl.BlockSpec((1, depth, part), lambda s, k: (s + first, k, 0))
    out_shape = [shape_of((rows, part))] * count
    out_specs = [pl.BlockSpec((rows, part), lambda s, k: (0, 0))] * count
    if with_split:
        operands = [factor] + ([] if pre is None else [pre]) + [a_high, a_low]
        once = pl.BlockSpec((rows, depth), lambda s, k: (0, jnp.where(s == 0, k, steps - 1)))
        in_specs = [once] * (len(operands) - 2) + [a_spec, a_spec]
        out_shape = [shape_of((rows, length), jnp.bfloat16)] * 2 + out_shape
        out_specs = [pl.BlockSpec((rows, length), lambda s, k: (0, 0))] * 2 + out_specs
    else:
        operands = [factor[0], factor[1], a_high, a_low]
        in_specs = [pl.BlockSpec((rows, depth), lambda s, k: (0, k))] * 2 + [a_spec, a_spec]
    got = order(
        functools.partial(product_kernel, count, steps, pre is not None, with_split),
        operands,
        in_specs,
        out_shape,
        out_specs,
        (count, steps),
        6 * rows * length * part * count,
        4 * length * part * count + 8 * rows * length,
        "products",
        scratch=[pltpu.VMEM((rows, part), jnp.float32)],
    )
    if with_split:
        return (got[0], got[1]), list(got[2:])
    return factor, list(got)


def elimination_kernel(sources, sizes, *refs):
    value = None
    for i in range(sources):
        c_high, c_low, f_high, f_low = (r[...] for r in refs[4 * i : 4 * i + 4])
        term = triple_dot(c_high, c_low, f_high, f_low)
        value = term if value is None else value + term
    start = 0
    for ref, size in zip(refs[4 * sources :], sizes):
        ref[...] = value[start : start + size]
        start += size


def elimination(order, pairs, sizes):
    operands = []
    for coupled, factor in pairs:
        operands += [*coupled, *factor]
    rows, depth = pairs[0][0][0].shape
    length = pairs[0][1][0].shape[1]
    tile = tile_of(length, 512)
    left = pl.BlockSpec((rows, depth), lambda i: (0, 0))
    right = pl.BlockSpec((depth, tile), lambda i: (0, i))
    return order(
        functools.partial(elimination_kernel, len(pairs), sizes),
        operands,
        [left, left, right, right] * len(pairs),
        [shape_of((size, length)) for size in sizes],
        [pl.BlockSpec((size, tile), lambda i: (0, i)) for size in sizes],
        (length // tile,),
        6 * rows * depth * length * len(pairs),
        4 * length * (rows + depth * len(pairs)),
        "elimination",
    )


def sum_kernel(sign, *refs):
    value = refs[0][...]
    for ref in refs[1:-1]:
        value = value + ref[...]
    refs[-1][...] = sign * value


def signed_sum(order, sign, terms):
    rows, width = terms[0].shape
    tile = tile_of(rows, 128)
    spec = pl.BlockSpec((tile, width), lambda i: (i, 0))
    size = rows * width
    return order(
        functools.partial(sum_kernel, sign), terms, [spec] * len(terms), shape_of((rows, width)), spec, (rows // tile,),
        len(terms) * size, 4 * (len(terms) + 1) * size, "signed_sum",
    )


def relay_kernel(in_ref, out_ref):
    out_ref[...] = in_ref[...]


def relay(order, value):
    block = (value.shape[0] // 2, *value.shape[1:])
    spec = pl.BlockSpec(block, lambda i: (i, 0, 0))
    return order(
        relay_kernel, [value], [spec], shape_of(value.shape), spec, (2,),
        value.size, 8 * value.size, "relay",
    )


def assembly_kernel(in_ref, *refs):
    out_ref = refs[-1]
    outer, inner, _, part = in_ref.shape
    for a in range(inner):
        for q in range(outer):
            out_ref[0, :, pl.ds((a * outer + q) * part, part)] = in_ref[q, a]


def assembled(order, value, chunk, shape, whole=None):
    j, lo, hi = chunk
    operands = [value] + ([] if whole is None else [whole])
    return order(
        assembly_kernel,
        operands,
        [pl.BlockSpec(value.shape, lambda i: (0, 0, 0, 0))]
        + [pl.BlockSpec(memory_space=pl.ANY)] * (len(operands) - 1),
        shape_of(shape),
        pl.BlockSpec((1, hi - lo, shape[2]), lambda i: (j, lo // (hi - lo), 0)),
        (1,),
        value.size,
        8 * value.size,
        "assembled",
        aliases={} if whole is None else {1: 0},
    )


def inner_kernel(lefts_n, rights_n, terms, *refs):
    lefts = [r[0] for r in refs[:lefts_n]]
    rights = refs[lefts_n : lefts_n + 2 * rights_n]
    out = refs[-1]

    @pl.when(pl.program_id(0) == 0)
    def _():
        out[...] = jnp.zeros_like(out)

    for which, right, row, column in terms:
        left = jnp.concatenate([lefts[a] for a in which], 0) if len(which) > 1 else lefts[which[0]]
        high, low = split_here(-left)
        value = triple_dot(high, low, rights[2 * right][...], rights[2 * right + 1][...], (1, 1))
        out[row : row + value.shape[0], column : column + value.shape[1]] += value


def inner_products(order, whole, lefts, rights, terms, shape, extra=()):
    length = whole.shape[2]
    depth = tile_of(length, 1024)
    flat = [part for right in rights for part in right]

    def left_spec(j, lo, hi):
        return pl.BlockSpec((1, hi - lo, depth), lambda k: (j, lo // (hi - lo), k))

    return order(
        functools.partial(inner_kernel, len(lefts), len(rights), terms),
        [whole] * len(lefts) + flat,
        [left_spec(*chunk) for chunk in lefts]
        + [pl.BlockSpec((v.shape[0], depth), lambda k: (0, k)) for v in flat],
        shape_of(shape),
        pl.BlockSpec(shape, lambda k: (0, 0)),
        (length // depth,),
        6 * shape[0] * shape[1] * length,
        sum(2 * v.size for v in flat),
        "inner_products",
        extra=extra,
    )


def finish_kernel(shares, cols_n, sizes, *refs):
    def total(first):
        value = refs[first][...]
        for ref in refs[first + 1 : first + shares]:
            value = value + ref[...]
        return value

    early, late, final = (total(shares * i) for i in range(3))
    base_cross, base_diag, cross, diag, place = refs[3 * shares :]
    wide = sum(sizes)
    cut = cols_n * sizes[0]
    place[0:2 * wide + sizes[0], :] = late
    place[2 * wide + sizes[0] : 3 * wide, :] = final

    def put(out, base, i, row):
        for c in range(cols_n):
            for start, first, size in ((0, 0, sizes[0]), (sizes[0], cut, sizes[1])):
                to = pl.ds(c * wide + start, size)
                out[i, :, to] = base[i, :, to] + place[row : row + wide, pl.ds(first + c * size, size)]

    diag[0] = base_diag[0] + early[:wide]
    cross[0] = base_cross[0] + early[wide : 2 * wide]
    diag[1] = base_diag[1] + early[2 * wide :]
    put(cross, base_cross, 1, 0)
    put(cross, base_cross, 2, wide)
    put(diag, base_diag, 2, 2 * wide)


def finish(order, early, late, final, base_cross, base_diag, cols_n, sizes):
    operands = early + late + final + [base_cross, base_diag]
    shape = base_cross.shape
    once = [pl.BlockSpec(v.shape, lambda i, n=v.ndim: (0,) * n) for v in operands]
    moved = 4 * sum(v.size for v in operands)
    return order(
        functools.partial(finish_kernel, len(early), cols_n, sizes),
        operands,
        once,
        [shape_of(shape)] * 2,
        [once[-1]] * 2,
        (1,),
        moved // 4,
        moved,
        "finish",
        scratch=[pltpu.VMEM((3 * shape[1], shape[2]), jnp.float32)],
    )


def shards(ainv, panels, pattern, coupling, dinv):
    rows_n = lax.axis_size("prow")
    cols_n = lax.axis_size("pcol")
    row = lax.axis_index("prow")
    col = lax.axis_index("pcol")
    local_rows, local_cols = panels.shape[1:]
    part = ainv.shape[1] // rows_n
    ratio = cols_n // rows_n
    blocks_here = local_rows // NB

    flags = lax.dynamic_slice_in_dim(pattern, row * blocks_here, blocks_here, 1)
    mask = jnp.repeat(flags.astype(jnp.float32), NB, axis=1)[:, None, :]
    turned = jnp.swapaxes(panels, 1, 2)

    cut = local_cols * 3 // 4
    chunks = [(0, 0, local_cols), (1, 0, local_cols), (2, 0, cut), (2, cut, local_cols)]
    last_cuts = [(0, cut), (cut, local_cols)]
    partner = row ^ jnp.arange(rows_n, dtype=jnp.int32)

    def columns(matrix, cuts):
        cube = matrix.reshape(matrix.shape[0], cols_n, local_cols)
        kept = [cube[:, :, lo:hi].reshape(matrix.shape[0], -1) for lo, hi in cuts]
        return split(jnp.concatenate(kept, 1).T)

    c_one = columns(coupling[0], [(0, local_cols)])
    c_two = columns(coupling[1], last_cuts)
    c_three = columns(coupling[2], last_cuts)

    def gather(shard):
        return lax.all_gather(shard, "pcol", axis=0, tiled=True)

    def send(pieces):
        return [exchange(p, "prow", rows_n, s + 1) for s, p in enumerate(pieces)]

    def to_columns(total):
        count = total.shape[0] // cols_n
        return lax.all_to_all(total.reshape(cols_n, count, part), "pcol", 0, 0)

    def to_rows(value):
        count = value.shape[1]
        value = value.reshape(rows_n, ratio * count, part)
        value = lax.all_to_all(value, "prow", 0, 0)
        return value.reshape(rows_n, ratio, count, part)

    def share(value):
        return [value] + [exchange(value, "prow", rows_n, s) for s in range(1, rows_n)]

    first, second, third = coupling[0], coupling[1], coupling[2]
    start = col * local_cols

    def own_rows(matrix):
        return lax.dynamic_slice_in_dim(matrix, start, local_cols, 0)

    def own_cols(matrix):
        return lax.dynamic_slice_in_dim(matrix, start, local_cols, 1)

    bridge = second - matmul(first, third)
    d0 = own_rows(dinv[0])
    d1 = own_rows(dinv[1])
    k0 = tdot(own_cols(first), dinv[0])
    k1 = tdot(own_cols(bridge), dinv[0])
    k2 = tdot(own_cols(third), dinv[1])
    base_cross = jnp.stack(
        [-matmul(d0, first), -matmul(d0, bridge), matmul(k0, bridge) - matmul(d1, third)], 0
    )
    base_diag = jnp.stack(
        [d0, d1 + matmul(k0, first), own_rows(dinv[2]) + matmul(k1, bridge) + matmul(k2, third)], 0
    )

    order = Order()
    shard = masked(order, turned, mask, *chunks[0], [])
    g0 = gather(shard)
    inverse = prepared(order, ainv, partner, rows_n, part)

    early_work = [c_one[0], c_two[0], c_three[0], base_cross, base_diag]
    shard = masked(order, turned, mask, *chunks[1], [g0] + early_work)
    g1 = gather(shard)
    f0, sent = products(order, g0, inverse, 0, rows_n)
    s0 = [sent[0]] + send(sent[1:])
    pre1 = elimination(order, [(c_one, f0)], [cols_n * local_cols])

    shard = masked(order, turned, mask, *chunks[2], [g1])
    g2 = gather(shard)
    f1, sent = products(order, g1, inverse, 0, rows_n, pre1[0])
    s1 = [sent[0]] + send(sent[1:])
    m0 = to_columns(signed_sum(order, -1.0, s0))
    pre2 = elimination(
        order, [(c_two, f0), (c_three, f1)], [cols_n * (hi - lo) for lo, hi in last_cuts]
    )

    shard = masked(order, turned, mask, *chunks[3], [g2])
    g3 = gather(shard)
    f2, sent = products(order, g2, inverse, 0, rows_n, pre2[0])
    s2 = [sent[0]] + send(sent[1:])
    m0 = to_rows(relay(order, m0))
    m1 = to_columns(signed_sum(order, -1.0, s1))

    f3, sent = products(order, g3, inverse, 1, rows_n, pre2[1])
    s3 = send(sent)
    whole = assembled(order, m0, chunks[0], turned.shape)
    m1 = to_rows(relay(order, m1))
    m2 = to_columns(signed_sum(order, -1.0, s2))
    _, own3 = products(order, f3, inverse, 0, 1)
    m3 = to_columns(signed_sum(order, -1.0, own3 + s3))
    whole = assembled(order, m1, chunks[1], turned.shape, whole)
    three = 3 * local_cols
    early = inner_products(
        order, whole, chunks[:2], [f0, f1], (((0,), 0, 0, 0), ((0, 1), 1, local_cols, 0)),
        (three, cols_n * local_cols),
    )
    early = share(early)
    m2 = to_rows(relay(order, m2))
    m3 = to_rows(relay(order, m3))
    whole = assembled(order, m2, chunks[2], turned.shape, whole)
    start = cols_n * cut
    late = inner_products(
        order, whole, chunks[:3], [f2, f3], (((0, 1, 2), 0, 0, 0), ((0, 1, 2), 1, 0, start)),
        (2 * local_cols + cut, cols_n * local_cols),
    )
    late = share(late)
    whole = assembled(order, m3, chunks[3], turned.shape, whole)
    final = inner_products(
        order, whole, chunks[3:], [f2, f3], (((0,), 0, 0, 0), ((0,), 1, 0, start)),
        (local_cols - cut, cols_n * local_cols),
        early[1:],
    )
    final = share(final)
    cross, diag = finish(order, early, late, final, base_cross, base_diag, cols_n, (cut, local_cols - cut))
    return (jnp.swapaxes(whole, 1, 2), cross, diag)


def solution(mesh):
    placed = (P("prow", "pcol"), P(None, "prow", "pcol"), P(), P(), P())
    return jax.shard_map(
        shards,
        mesh=mesh,
        in_specs=placed,
        out_specs=(P(None, "prow", "pcol"), P(None, "pcol", None), P(None, "pcol", None)),
        check_vma=False,
    )
```

```python
import functools

import jax
import jax.numpy as jnp
from jax import lax
from jax.experimental import pallas as pl
from jax.experimental.pallas import tpu as pltpu
from jax.sharding import PartitionSpec as P

NB = 128
MIB = 1024 * 1024

precise = lax.Precision.HIGHEST


def matmul(left, right):
    return jnp.dot(left, right, precision=precise, preferred_element_type=jnp.float32)


def tdot(left, right):
    return lax.dot_general(
        left, right, (((0,), (0,)), ((), ())), precision=precise, preferred_element_type=jnp.float32
    )


def tile_of(size, wanted):
    return wanted if size % wanted == 0 else size


def split(values):
    high = lax.reduce_precision(values, exponent_bits=8, mantissa_bits=7)
    return high.astype(jnp.bfloat16), (values - high).astype(jnp.bfloat16)


def split_here(values):
    high = values.astype(jnp.bfloat16)
    return high, (values - high.astype(jnp.float32)).astype(jnp.bfloat16)


def triple_dot(left, right_high, right_low, contract=(1, 0)):
    dims = (((contract[0],), (contract[1],)), ((), ()))
    rows = left.shape[0] // 2
    wide = lax.dot_general(left, right_high, dims, preferred_element_type=jnp.float32)
    cross = lax.dot_general(left[:rows], right_low, dims, preferred_element_type=jnp.float32)
    return wide[:rows] + wide[rows:] + cross


def exchange(value, axis, size, step):
    return lax.ppermute(value, axis, [(i, i ^ step) for i in range(size)])


class Order:
    def __init__(self):
        self.last = None

    def __call__(self, kernel, operands, in_specs, out_shape, out_specs, grid, flops, moved,
                 name, scratch=(), limit=56, prefetch=(), extra=(), aliases=None):
        tokens = list(extra) + ([] if self.last is None else [self.last])
        skip = len(prefetch) + len(operands)

        def body(*refs):
            kernel(*refs[:skip], *refs[skip + len(tokens):])

        got = pl.pallas_call(
            body,
            out_shape=out_shape,
            grid_spec=pltpu.PrefetchScalarGridSpec(
                num_scalar_prefetch=len(prefetch),
                grid=grid,
                in_specs=list(in_specs) + [pl.BlockSpec(memory_space=pl.ANY)] * len(tokens),
                out_specs=out_specs,
                scratch_shapes=list(scratch),
            ),
            compiler_params=pltpu.CompilerParams(vmem_limit_bytes=limit * MIB),
            cost_estimate=pl.CostEstimate(
                flops=flops // 16, bytes_accessed=moved // 16, transcendentals=0
            ),
            input_output_aliases=aliases or {},
            name=name,
        )(*prefetch, *operands, *tokens)
        self.last = got[0] if isinstance(got, (tuple, list)) else got
        return got


def shape_of(shape, dtype=jnp.float32):
    return jax.ShapeDtypeStruct(shape, dtype)


def mask_kernel(panel_ref, mask_ref, out_ref):
    out_ref[...] = panel_ref[0] * mask_ref[0]


def masked(order, panels, mask, j, lo, hi, extra):
    rows = panels.shape[2]
    count = hi - lo
    return order(
        mask_kernel,
        [panels, mask],
        [
            pl.BlockSpec((1, count, rows), lambda i: (j, lo // count, 0)),
            pl.BlockSpec((1, 1, rows), lambda i: (j, 0, 0)),
        ],
        shape_of((count, rows)),
        pl.BlockSpec((count, rows), lambda i: (0, 0)),
        (1,),
        count * rows,
        8 * count * rows,
        "masked",
        extra=extra,
    )


def prepare_kernel(partner_ref, a_ref, high_ref, low_ref):
    high_ref[0], low_ref[0] = split_here(a_ref[...])


def prepared(order, ainv, partner, count, part):
    rows = ainv.shape[0]
    if part % 128:
        pieces = [
            split(lax.dynamic_slice_in_dim(ainv, partner[s] * part, part, 1)) for s in range(count)
        ]
        return jnp.stack([p[0] for p in pieces], 0), jnp.stack([p[1] for p in pieces], 0)
    tile = tile_of(rows, 1024)
    shape = shape_of((count, rows, part), jnp.bfloat16)
    spec = pl.BlockSpec((1, tile, part), lambda s, i, partner: (s, i, 0))
    return order(
        prepare_kernel,
        [ainv],
        [pl.BlockSpec((tile, part), lambda s, i, partner: (i, partner[s]))],
        (shape, shape),
        (spec, spec),
        (count, rows // tile),
        4 * ainv.size,
        8 * ainv.size,
        "prepared",
        prefetch=[partner],
    )


def product_kernel(count, steps, with_pre, with_split, *refs):
    refs = list(refs)
    s, k = pl.program_id(0), pl.program_id(1)
    if with_split:
        gathered_ref = refs.pop(0)
        pre_ref = refs.pop(0) if with_pre else None
        a_high_ref, a_low_ref = refs.pop(0), refs.pop(0)
        factor_ref = refs.pop(0)
        rows, depth = gathered_ref.shape
        here = pl.ds(pl.multiple_of(k * depth, depth), depth)

        @pl.when(s == 0)
        def _():
            strip = 16

            @pl.loop(0, rows // strip)
            def _(i):
                first = pl.multiple_of(i * strip, strip)
                values = gathered_ref[pl.ds(first, strip), :]
                if with_pre:
                    values = values - pre_ref[pl.ds(first, strip), :]
                high, low = split_here(values)
                factor_ref[pl.ds(first, strip), here] = high
                factor_ref[pl.ds(pl.multiple_of(first + rows, strip), strip), here] = low

        factor = factor_ref[:, here]
    else:
        factor_ref, a_high_ref, a_low_ref = refs[:3]
        refs = refs[3:]
        factor = factor_ref[...]
    outs, total_ref = refs[:count], refs[count]
    value = triple_dot(factor, a_high_ref[0], a_low_ref[0])

    @pl.when(k == 0)
    def _():
        total_ref[...] = value

    @pl.when(k > 0)
    def _():
        total_ref[...] += value

    for i in range(count):
        @pl.when((s == i) & (k == steps - 1))
        def _():
            outs[i][...] = total_ref[...]


def products(order, factor, inverse, first, last, pre=None):
    with_split = factor.dtype == jnp.float32
    a_high, a_low = inverse
    count = last - first
    part = a_high.shape[2]
    rows, length = factor.shape
    rows = rows if with_split else rows // 2
    depth = tile_of(length, 1024)
    steps = length // depth
    a_spec = pl.BlockSpec((1, depth, part), lambda s, k: (s + first, k, 0))
    out_shape = [shape_of((rows, part))] * count
    out_specs = [pl.BlockSpec((rows, part), lambda s, k: (0, 0))] * count
    if with_split:
        operands = [factor] + ([] if pre is None else [pre]) + [a_high, a_low]
        once = pl.BlockSpec((rows, depth), lambda s, k: (0, jnp.where(s == 0, k, steps - 1)))
        in_specs = [once] * (len(operands) - 2) + [a_spec, a_spec]
        out_shape = [shape_of((2 * rows, length), jnp.bfloat16)] + out_shape
        out_specs = [pl.BlockSpec((2 * rows, length), lambda s, k: (0, 0))] + out_specs
    else:
        operands = [factor, a_high, a_low]
        in_specs = [pl.BlockSpec((2 * rows, depth), lambda s, k: (0, k)), a_spec, a_spec]
    got = order(
        functools.partial(product_kernel, count, steps, pre is not None, with_split),
        operands,
        in_specs,
        out_shape,
        out_specs,
        (count, steps),
        6 * rows * length * part * count,
        4 * length * part * count + 8 * rows * length,
        "products",
        scratch=[pltpu.VMEM((rows, part), jnp.float32)],
    )
    if with_split:
        return got[0], list(got[1:])
    return factor, list(got)


def elimination_kernel(sources, sizes, *refs):
    value = None
    for i in range(sources):
        coupled, factor_ref = refs[2 * i][...], refs[2 * i + 1]
        depth = factor_ref.shape[0] // 2
        term = triple_dot(coupled, factor_ref[:depth, :], factor_ref[depth:, :])
        value = term if value is None else value + term
    start = 0
    for ref, size in zip(refs[2 * sources :], sizes):
        ref[...] = value[start : start + size]
        start += size


def elimination(order, pairs, sizes):
    operands = [value for pair in pairs for value in pair]
    rows, depth = pairs[0][0].shape[0] // 2, pairs[0][0].shape[1]
    length = pairs[0][1].shape[1]
    tile = tile_of(length, 512)
    left = pl.BlockSpec((2 * rows, depth), lambda i: (0, 0))
    right = pl.BlockSpec((2 * depth, tile), lambda i: (0, i))
    return order(
        functools.partial(elimination_kernel, len(pairs), sizes),
        operands,
        [left, right] * len(pairs),
        [shape_of((size, length)) for size in sizes],
        [pl.BlockSpec((size, tile), lambda i: (0, i)) for size in sizes],
        (length // tile,),
        6 * rows * depth * length * len(pairs),
        4 * length * (rows + depth * len(pairs)),
        "elimination",
    )


def sum_kernel(shares, *refs):
    out = refs[-1]
    start = 0
    for i in range(0, len(refs) - 1, shares):
        value = refs[i][...]
        for ref in refs[i + 1 : i + shares]:
            value = value + ref[...]
        out[0, start : start + value.shape[0], :] = -value
        start += value.shape[0]


def negative_sums(order, groups, cols_n):
    flat = [value for group in groups for value in group]
    width = flat[0].shape[1]
    counts = [group[0].shape[0] // cols_n for group in groups]
    shape = (cols_n, sum(counts), width)
    return order(
        functools.partial(sum_kernel, len(groups[0])),
        flat,
        [pl.BlockSpec((v.shape[0] // cols_n, width), lambda i: (i, 0)) for v in flat],
        shape_of(shape),
        pl.BlockSpec((1, sum(counts), width), lambda i: (i, 0, 0)),
        (cols_n,),
        sum(v.size for v in flat),
        4 * sum(v.size for v in flat),
        "negative_sums",
    )


def relay_kernel(in_ref, out_ref):
    out_ref[...] = in_ref[...]


def relay(order, value):
    block = (value.shape[0] // 2, *value.shape[1:])
    spec = pl.BlockSpec(block, lambda i: (i, 0, 0))
    return order(
        relay_kernel, [value], [spec], shape_of(value.shape), spec, (2,),
        value.size, 8 * value.size, "relay",
    )


def assembly_kernel(in_ref, *refs):
    out_ref = refs[-1]
    outer, inner, _, part = in_ref.shape
    count = out_ref.shape[1]
    for i in range(out_ref.shape[0]):
        for a in range(inner):
            for q in range(outer):
                to = pl.ds((a * outer + q) * part, part)
                out_ref[i, :, to] = in_ref[q, a, i * count : (i + 1) * count, :]


def assembled(order, value, chunks, shape, whole=None):
    j, lo, hi = chunks[0]
    operands = [value] + ([] if whole is None else [whole])
    return order(
        assembly_kernel,
        operands,
        [pl.BlockSpec(value.shape, lambda i: (0, 0, 0, 0))]
        + [pl.BlockSpec(memory_space=pl.ANY)] * (len(operands) - 1),
        shape_of(shape),
        pl.BlockSpec((len(chunks), hi - lo, shape[2]), lambda i: (j, lo // (hi - lo), 0)),
        (1,),
        value.size,
        8 * value.size,
        "assembled",
        aliases={} if whole is None else {1: 0},
    )


def inner_kernel(lefts_n, rights_n, terms, *refs):
    lefts = [r[0] for r in refs[:lefts_n]]
    rights = refs[lefts_n : lefts_n + rights_n]
    out = refs[-1]

    @pl.when(pl.program_id(0) == 0)
    def _():
        out[...] = jnp.zeros_like(out)

    for which, right, row, column in terms:
        left = jnp.concatenate([lefts[a] for a in which], 0) if len(which) > 1 else lefts[which[0]]
        stacked = jnp.concatenate(split_here(-left), 0)
        half = rights[right].shape[0] // 2
        value = triple_dot(stacked, rights[right][:half], rights[right][half:], (1, 1))
        out[row : row + value.shape[0], column : column + value.shape[1]] += value


def inner_products(order, whole, lefts, rights, terms, shape, extra=()):
    length = whole.shape[2]
    depth = tile_of(length, 1024)

    def left_spec(j, lo, hi):
        return pl.BlockSpec((1, hi - lo, depth), lambda k: (j, lo // (hi - lo), k))

    return order(
        functools.partial(inner_kernel, len(lefts), len(rights), terms),
        [whole] * len(lefts) + list(rights),
        [left_spec(*chunk) for chunk in lefts]
        + [pl.BlockSpec((v.shape[0], depth), lambda k: (0, k)) for v in rights],
        shape_of(shape),
        pl.BlockSpec(shape, lambda k: (0, 0)),
        (length // depth,),
        6 * shape[0] * shape[1] * length,
        sum(2 * v.size for v in rights),
        "inner_products",
        extra=extra,
    )


def finish_kernel(shares, cols_n, sizes, *refs):
    def total(first):
        value = refs[first][...]
        for ref in refs[first + 1 : first + shares]:
            value = value + ref[...]
        return value

    early, late, final = (total(shares * i) for i in range(3))
    base_cross, base_diag, cross, diag, place = refs[3 * shares :]
    wide = sum(sizes)
    cut = cols_n * sizes[0]
    place[0:2 * wide + sizes[0], :] = late
    place[2 * wide + sizes[0] : 3 * wide, :] = final

    def put(out, base, i, row):
        for c in range(cols_n):
            for start, first, size in ((0, 0, sizes[0]), (sizes[0], cut, sizes[1])):
                to = pl.ds(c * wide + start, size)
                out[i, :, to] = base[i, :, to] + place[row : row + wide, pl.ds(first + c * size, size)]

    diag[0] = base_diag[0] + early[:wide]
    cross[0] = base_cross[0] + early[wide : 2 * wide]
    diag[1] = base_diag[1] + early[2 * wide :]
    put(cross, base_cross, 1, 0)
    put(cross, base_cross, 2, wide)
    put(diag, base_diag, 2, 2 * wide)


def finish(order, early, late, final, base_cross, base_diag, cols_n, sizes):
    operands = early + late + final + [base_cross, base_diag]
    shape = base_cross.shape
    once = [pl.BlockSpec(v.shape, lambda i, n=v.ndim: (0,) * n) for v in operands]
    moved = 4 * sum(v.size for v in operands)
    return order(
        functools.partial(finish_kernel, len(early), cols_n, sizes),
        operands,
        once,
        [shape_of(shape)] * 2,
        [once[-1]] * 2,
        (1,),
        moved // 4,
        moved,
        "finish",
        scratch=[pltpu.VMEM((3 * shape[1], shape[2]), jnp.float32)],
    )


def shards(ainv, panels, pattern, coupling, dinv):
    rows_n = lax.axis_size("prow")
    cols_n = lax.axis_size("pcol")
    row = lax.axis_index("prow")
    col = lax.axis_index("pcol")
    local_rows, local_cols = panels.shape[1:]
    part = ainv.shape[1] // rows_n
    ratio = cols_n // rows_n
    blocks_here = local_rows // NB

    flags = lax.dynamic_slice_in_dim(pattern, row * blocks_here, blocks_here, 1)
    mask = jnp.repeat(flags.astype(jnp.float32), NB, axis=1)[:, None, :]
    turned = jnp.swapaxes(panels, 1, 2)

    cut = local_cols * 3 // 4
    chunks = [(0, 0, local_cols), (1, 0, local_cols), (2, 0, cut), (2, cut, local_cols)]
    last_cuts = [(0, cut), (cut, local_cols)]
    partner = row ^ jnp.arange(rows_n, dtype=jnp.int32)

    def columns(matrix, cuts):
        cube = matrix.reshape(matrix.shape[0], cols_n, local_cols)
        kept = [cube[:, :, lo:hi].reshape(matrix.shape[0], -1) for lo, hi in cuts]
        return jnp.concatenate(split(jnp.concatenate(kept, 1).T), 0)

    c_one = columns(coupling[0], [(0, local_cols)])
    c_two = columns(coupling[1], last_cuts)
    c_three = columns(coupling[2], last_cuts)

    def gather(shard):
        return lax.all_gather(shard, "pcol", axis=0, tiled=True)

    def send(pieces):
        return [exchange(p, "prow", rows_n, s + 1) for s, p in enumerate(pieces)]

    def to_columns(groups):
        return lax.all_to_all(negative_sums(order, groups, cols_n), "pcol", 0, 0)

    def to_rows(value):
        count = value.shape[1]
        value = value.reshape(rows_n, ratio * count, part)
        value = lax.all_to_all(value, "prow", 0, 0)
        return value.reshape(rows_n, ratio, count, part)

    def share(value):
        return [value] + [exchange(value, "prow", rows_n, s) for s in range(1, rows_n)]

    first, second, third = coupling[0], coupling[1], coupling[2]
    start = col * local_cols

    def own_rows(matrix):
        return lax.dynamic_slice_in_dim(matrix, start, local_cols, 0)

    def own_cols(matrix):
        return lax.dynamic_slice_in_dim(matrix, start, local_cols, 1)

    bridge = second - matmul(first, third)
    d0 = own_rows(dinv[0])
    d1 = own_rows(dinv[1])
    k0 = tdot(own_cols(first), dinv[0])
    k1 = tdot(own_cols(bridge), dinv[0])
    k2 = tdot(own_cols(third), dinv[1])
    base_cross = jnp.stack(
        [-matmul(d0, first), -matmul(d0, bridge), matmul(k0, bridge) - matmul(d1, third)], 0
    )
    base_diag = jnp.stack(
        [d0, d1 + matmul(k0, first), own_rows(dinv[2]) + matmul(k1, bridge) + matmul(k2, third)], 0
    )

    order = Order()
    shard = masked(order, turned, mask, *chunks[0], [])
    g0 = gather(shard)
    inverse = prepared(order, ainv, partner, rows_n, part)

    early_work = [c_one, c_two, c_three, base_cross, base_diag]
    shard = masked(order, turned, mask, *chunks[1], [g0] + early_work)
    g1 = gather(shard)
    f0, sent = products(order, g0, inverse, 0, rows_n)
    s0 = [sent[0]] + send(sent[1:])
    pre1 = elimination(order, [(c_one, f0)], [cols_n * local_cols])

    shard = masked(order, turned, mask, *chunks[2], [g1])
    g2 = gather(shard)
    f1, sent = products(order, g1, inverse, 0, rows_n, pre1[0])
    s1 = [sent[0]] + send(sent[1:])
    pre2 = elimination(
        order, [(c_two, f0), (c_three, f1)], [cols_n * (hi - lo) for lo, hi in last_cuts]
    )

    shard = masked(order, turned, mask, *chunks[3], [g2])
    g3 = gather(shard)
    f2, sent = products(order, g2, inverse, 0, rows_n, pre2[0])
    s2 = [sent[0]] + send(sent[1:])
    m01 = to_columns([s0, s1])

    f3, sent = products(order, g3, inverse, 1, rows_n, pre2[1])
    s3 = send(sent)
    m2 = to_columns([s2])
    _, own3 = products(order, f3, inverse, 0, 1)
    m01 = to_rows(relay(order, m01))
    m3 = to_columns([own3 + s3])
    m2 = to_rows(relay(order, m2))
    whole = assembled(order, m01, chunks[:2], turned.shape)
    three = 3 * local_cols
    early = inner_products(
        order, whole, chunks[:2], [f0, f1], (((0,), 0, 0, 0), ((0, 1), 1, local_cols, 0)),
        (three, cols_n * local_cols),
    )
    early = share(early)
    m3 = to_rows(relay(order, m3))
    whole = assembled(order, m2, chunks[2:3], turned.shape, whole)
    start = cols_n * cut
    late = inner_products(
        order, whole, chunks[:3], [f2, f3], (((0, 1, 2), 0, 0, 0), ((0, 1, 2), 1, 0, start)),
        (2 * local_cols + cut, cols_n * local_cols),
    )
    late = share(late)
    whole = assembled(order, m3, chunks[3:], turned.shape, whole)
    final = inner_products(
        order, whole, chunks[3:], [f2, f3], (((0,), 0, 0, 0), ((0,), 1, 0, start)),
        (local_cols - cut, cols_n * local_cols),
        early[1:],
    )
    final = share(final)
    cross, diag = finish(order, early, late, final, base_cross, base_diag, cols_n, (cut, local_cols - cut))
    return (jnp.swapaxes(whole, 1, 2), cross, diag)


def solution(mesh):
    placed = (P("prow", "pcol"), P(None, "prow", "pcol"), P(), P(), P())
    return jax.shard_map(
        shards,
        mesh=mesh,
        in_specs=placed,
        out_specs=(P(None, "prow", "pcol"), P(None, "pcol", None), P(None, "pcol", None)),
        check_vma=False,
    )
```

```python
import functools

import jax
import jax.numpy as jnp
from jax import lax
from jax.experimental import pallas as pl
from jax.experimental.pallas import tpu as pltpu
from jax.sharding import PartitionSpec as P

NB = 128
MIB = 1024 * 1024

precise = lax.Precision.HIGHEST


def matmul(left, right):
    return jnp.dot(left, right, precision=precise, preferred_element_type=jnp.float32)


def tdot(left, right):
    return lax.dot_general(
        left, right, (((0,), (0,)), ((), ())), precision=precise, preferred_element_type=jnp.float32
    )


def tile_of(size, wanted):
    return wanted if size % wanted == 0 else size


def split(values):
    high = lax.reduce_precision(values, exponent_bits=8, mantissa_bits=7)
    return high.astype(jnp.bfloat16), (values - high).astype(jnp.bfloat16)


def split_here(values):
    high = values.astype(jnp.bfloat16)
    return high, (values - high.astype(jnp.float32)).astype(jnp.bfloat16)


def triple_dot(left, right_high, right_low, contract=(1, 0)):
    dims = (((contract[0],), (contract[1],)), ((), ()))
    rows = left.shape[0] // 2
    wide = lax.dot_general(left, right_high, dims, preferred_element_type=jnp.float32)
    cross = lax.dot_general(left[:rows], right_low, dims, preferred_element_type=jnp.float32)
    return wide[:rows] + wide[rows:] + cross


def exchange(value, axis, size, step):
    return lax.ppermute(value, axis, [(i, i ^ step) for i in range(size)])


class Order:
    def __init__(self):
        self.last = None

    def __call__(self, kernel, operands, in_specs, out_shape, out_specs, grid, flops, moved,
                 name, scratch=(), limit=56, prefetch=(), extra=(), aliases=None):
        tokens = list(extra) + ([] if self.last is None else [self.last])
        skip = len(prefetch) + len(operands)

        def body(*refs):
            kernel(*refs[:skip], *refs[skip + len(tokens):])

        got = pl.pallas_call(
            body,
            out_shape=out_shape,
            grid_spec=pltpu.PrefetchScalarGridSpec(
                num_scalar_prefetch=len(prefetch),
                grid=grid,
                in_specs=list(in_specs) + [pl.BlockSpec(memory_space=pl.ANY)] * len(tokens),
                out_specs=out_specs,
                scratch_shapes=list(scratch),
            ),
            compiler_params=pltpu.CompilerParams(vmem_limit_bytes=limit * MIB),
            cost_estimate=pl.CostEstimate(
                flops=flops // 16, bytes_accessed=moved // 16, transcendentals=0
            ),
            input_output_aliases=aliases or {},
            name=name,
        )(*prefetch, *operands, *tokens)
        self.last = got[0] if isinstance(got, (tuple, list)) else got
        return got


def shape_of(shape, dtype=jnp.float32):
    return jax.ShapeDtypeStruct(shape, dtype)


def mask_kernel(panel_ref, mask_ref, out_ref):
    out_ref[...] = panel_ref[0] * mask_ref[0]


def masked(order, panels, mask, j, lo, hi, extra):
    rows = panels.shape[2]
    count = hi - lo
    return order(
        mask_kernel,
        [panels, mask],
        [
            pl.BlockSpec((1, count, rows), lambda i: (j, lo // count, 0)),
            pl.BlockSpec((1, 1, rows), lambda i: (j, 0, 0)),
        ],
        shape_of((count, rows)),
        pl.BlockSpec((count, rows), lambda i: (0, 0)),
        (1,),
        count * rows,
        8 * count * rows,
        "masked",
        extra=extra,
    )


def prepare_kernel(partner_ref, a_ref, high_ref, low_ref):
    high_ref[0], low_ref[0] = split_here(a_ref[...])


def prepared(order, ainv, partner, count, part):
    rows = ainv.shape[0]
    if part % 128:
        pieces = [
            split(lax.dynamic_slice_in_dim(ainv, partner[s] * part, part, 1)) for s in range(count)
        ]
        return jnp.stack([p[0] for p in pieces], 0), jnp.stack([p[1] for p in pieces], 0)
    tile = tile_of(rows, 1024)
    shape = shape_of((count, rows, part), jnp.bfloat16)
    spec = pl.BlockSpec((1, tile, part), lambda s, i, partner: (s, i, 0))
    return order(
        prepare_kernel,
        [ainv],
        [pl.BlockSpec((tile, part), lambda s, i, partner: (i, partner[s]))],
        (shape, shape),
        (spec, spec),
        (count, rows // tile),
        4 * ainv.size,
        8 * ainv.size,
        "prepared",
        prefetch=[partner],
    )


def product_kernel(count, steps, with_pre, with_split, *refs):
    refs = list(refs)
    s, k = pl.program_id(0), pl.program_id(1)
    if with_split:
        gathered_ref = refs.pop(0)
        pre_ref = refs.pop(0) if with_pre else None
        a_high_ref, a_low_ref = refs.pop(0), refs.pop(0)
        factor_ref = refs.pop(0)
        rows, depth = gathered_ref.shape
        here = pl.ds(pl.multiple_of(k * depth, depth), depth)

        @pl.when(s == 0)
        def _():
            strip = 16

            @pl.loop(0, rows // strip)
            def _(i):
                first = pl.multiple_of(i * strip, strip)
                values = gathered_ref[pl.ds(first, strip), :]
                if with_pre:
                    values = values - pre_ref[pl.ds(first, strip), :]
                high, low = split_here(values)
                factor_ref[pl.ds(first, strip), here] = high
                factor_ref[pl.ds(pl.multiple_of(first + rows, strip), strip), here] = low

        factor = factor_ref[:, here]
    else:
        factor_ref, a_high_ref, a_low_ref = refs[:3]
        refs = refs[3:]
        factor = factor_ref[...]
    outs, total_ref = refs[:count], refs[count]
    value = triple_dot(factor, a_high_ref[0], a_low_ref[0])

    @pl.when(k == 0)
    def _():
        total_ref[...] = value

    @pl.when(k > 0)
    def _():
        total_ref[...] += value

    for i in range(count):
        @pl.when((s == i) & (k == steps - 1))
        def _():
            outs[i][...] = total_ref[...]


def products(order, factor, inverse, first, last, pre=None):
    with_split = factor.dtype == jnp.float32
    a_high, a_low = inverse
    count = last - first
    part = a_high.shape[2]
    rows, length = factor.shape
    rows = rows if with_split else rows // 2
    depth = tile_of(length, 2048)
    steps = length // depth
    a_spec = pl.BlockSpec((1, depth, part), lambda s, k: (s + first, k, 0))
    out_shape = [shape_of((rows, part))] * count
    out_specs = [pl.BlockSpec((rows, part), lambda s, k: (0, 0))] * count
    if with_split:
        operands = [factor] + ([] if pre is None else [pre]) + [a_high, a_low]
        once = pl.BlockSpec((rows, depth), lambda s, k: (0, jnp.where(s == 0, k, steps - 1)))
        in_specs = [once] * (len(operands) - 2) + [a_spec, a_spec]
        out_shape = [shape_of((2 * rows, length), jnp.bfloat16)] + out_shape
        out_specs = [pl.BlockSpec((2 * rows, length), lambda s, k: (0, 0))] + out_specs
    else:
        operands = [factor, a_high, a_low]
        in_specs = [pl.BlockSpec((2 * rows, depth), lambda s, k: (0, k)), a_spec, a_spec]
    got = order(
        functools.partial(product_kernel, count, steps, pre is not None, with_split),
        operands,
        in_specs,
        out_shape,
        out_specs,
        (count, steps),
        6 * rows * length * part * count,
        4 * length * part * count + 8 * rows * length,
        "products",
        scratch=[pltpu.VMEM((rows, part), jnp.float32)],
    )
    if with_split:
        return got[0], list(got[1:])
    return factor, list(got)


def elimination_kernel(sources, sizes, *refs):
    value = None
    for i in range(sources):
        coupled, factor_ref = refs[2 * i][...], refs[2 * i + 1]
        depth = factor_ref.shape[0] // 2
        term = triple_dot(coupled, factor_ref[:depth, :], factor_ref[depth:, :])
        value = term if value is None else value + term
    start = 0
    for ref, size in zip(refs[2 * sources :], sizes):
        ref[...] = value[start : start + size]
        start += size


def elimination(order, pairs, sizes):
    operands = [value for pair in pairs for value in pair]
    rows, depth = pairs[0][0].shape[0] // 2, pairs[0][0].shape[1]
    length = pairs[0][1].shape[1]
    tile = tile_of(length, 512)
    left = pl.BlockSpec((2 * rows, depth), lambda i: (0, 0))
    right = pl.BlockSpec((2 * depth, tile), lambda i: (0, i))
    return order(
        functools.partial(elimination_kernel, len(pairs), sizes),
        operands,
        [left, right] * len(pairs),
        [shape_of((size, length)) for size in sizes],
        [pl.BlockSpec((size, tile), lambda i: (0, i)) for size in sizes],
        (length // tile,),
        6 * rows * depth * length * len(pairs),
        4 * length * (rows + depth * len(pairs)),
        "elimination",
    )


def sum_kernel(shares, *refs):
    out = refs[-1]
    start = 0
    for i in range(0, len(refs) - 1, shares):
        value = refs[i][...]
        for ref in refs[i + 1 : i + shares]:
            value = value + ref[...]
        out[0, start : start + value.shape[0], :] = -value
        start += value.shape[0]


def negative_sums(order, groups, cols_n):
    flat = [value for group in groups for value in group]
    width = flat[0].shape[1]
    counts = [group[0].shape[0] // cols_n for group in groups]
    shape = (cols_n, sum(counts), width)
    return order(
        functools.partial(sum_kernel, len(groups[0])),
        flat,
        [pl.BlockSpec((v.shape[0] // cols_n, width), lambda i: (i, 0)) for v in flat],
        shape_of(shape),
        pl.BlockSpec((1, sum(counts), width), lambda i: (i, 0, 0)),
        (cols_n,),
        sum(v.size for v in flat),
        4 * sum(v.size for v in flat),
        "negative_sums",
    )


def relay_kernel(*refs):
    start = 0
    for ref in refs[:-1]:
        refs[-1][:, start : start + ref.shape[1], :] = ref[...]
        start += ref.shape[1]


def relay(order, *values):
    outer, _, width = values[0].shape
    counts = [v.shape[1] for v in values]
    half = outer // 2
    return order(
        relay_kernel,
        list(values),
        [pl.BlockSpec((half, n, width), lambda i: (i, 0, 0)) for n in counts],
        shape_of((outer, sum(counts), width)),
        pl.BlockSpec((half, sum(counts), width), lambda i: (i, 0, 0)),
        (2,),
        sum(v.size for v in values),
        8 * sum(v.size for v in values),
        "relay",
    )


def assembly_kernel(in_ref, *refs):
    out_ref = refs[-1]
    outer, inner, _, part = in_ref.shape
    for a in range(inner):
        for q in range(outer):
            out_ref[0, :, pl.ds((a * outer + q) * part, part)] = in_ref[q, a]


def assembled(order, value, j, shape, whole=None):
    operands = [value] + ([] if whole is None else [whole])
    return order(
        assembly_kernel,
        operands,
        [pl.BlockSpec(value.shape, lambda i: (0, 0, 0, 0))]
        + [pl.BlockSpec(memory_space=pl.ANY)] * (len(operands) - 1),
        shape_of(shape),
        pl.BlockSpec((1, *shape[1:]), lambda i: (j, 0, 0)),
        (1,),
        value.size,
        8 * value.size,
        "assembled",
        aliases={} if whole is None else {1: 0},
    )


def inner_kernel(terms, *refs):
    out = refs[-1]

    @pl.when(pl.program_id(0) == 0)
    def _():
        out[...] = jnp.zeros_like(out)

    stacked = jnp.concatenate(split_here(-refs[0][0]), 0)
    for right, (row, column) in zip(refs[1:-1], terms):
        half = right.shape[0] // 2
        value = triple_dot(stacked, right[:half], right[half:], (1, 1))
        out[row : row + value.shape[0], column : column + half] += value


def inner_products(order, whole, j, rights, terms, shape, extra=()):
    _, count, length = whole.shape
    depth = tile_of(length, 1024)
    return order(
        functools.partial(inner_kernel, terms),
        [whole] + list(rights),
        [pl.BlockSpec((1, count, depth), lambda k: (j, 0, k))]
        + [pl.BlockSpec((v.shape[0], depth), lambda k: (0, k)) for v in rights],
        shape_of(shape),
        pl.BlockSpec(shape, lambda k: (0, 0)),
        (length // depth,),
        6 * shape[0] * shape[1] * length,
        sum(2 * v.size for v in rights),
        "inner_products",
        extra=extra,
    )


def finish_kernel(shares, cols_n, sizes, *refs):
    def total(first):
        value = refs[first][...]
        for ref in refs[first + 1 : first + shares]:
            value = value + ref[...]
        return value

    one, two, three = (total(shares * i) for i in range(3))
    base_cross, base_diag, cross, diag, place = refs[3 * shares :]
    wide = sum(sizes)
    cut = cols_n * sizes[0]
    place[:wide, :] = one[2 * wide :]
    place[wide : 2 * wide, :] = two[wide:]
    place[2 * wide :, :] = three

    def put(out, base, i, row):
        for c in range(cols_n):
            for start, first, size in ((0, 0, sizes[0]), (sizes[0], cut, sizes[1])):
                to = pl.ds(c * wide + start, size)
                out[i, :, to] = base[i, :, to] + place[row : row + wide, pl.ds(first + c * size, size)]

    diag[0] = base_diag[0] + one[:wide]
    cross[0] = base_cross[0] + one[wide : 2 * wide]
    diag[1] = base_diag[1] + two[:wide]
    put(cross, base_cross, 1, 0)
    put(cross, base_cross, 2, wide)
    put(diag, base_diag, 2, 2 * wide)


def finish(order, one, two, three, base_cross, base_diag, cols_n, sizes):
    operands = one + two + three + [base_cross, base_diag]
    shape = base_cross.shape
    once = [pl.BlockSpec(v.shape, lambda i, n=v.ndim: (0,) * n) for v in operands]
    moved = 4 * sum(v.size for v in operands)
    return order(
        functools.partial(finish_kernel, len(one), cols_n, sizes),
        operands,
        once,
        [shape_of(shape)] * 2,
        [once[-1]] * 2,
        (1,),
        moved // 4,
        moved,
        "finish",
        scratch=[pltpu.VMEM((3 * shape[1], shape[2]), jnp.float32)],
    )


def shards(ainv, panels, pattern, coupling, dinv):
    rows_n = lax.axis_size("prow")
    cols_n = lax.axis_size("pcol")
    row = lax.axis_index("prow")
    col = lax.axis_index("pcol")
    local_rows, local_cols = panels.shape[1:]
    part = ainv.shape[1] // rows_n
    ratio = cols_n // rows_n
    blocks_here = local_rows // NB

    flags = lax.dynamic_slice_in_dim(pattern, row * blocks_here, blocks_here, 1)
    mask = jnp.repeat(flags.astype(jnp.float32), NB, axis=1)[:, None, :]
    turned = jnp.swapaxes(panels, 1, 2)

    cut = local_cols * 3 // 4
    chunks = [(0, 0, local_cols), (1, 0, local_cols), (2, 0, cut), (2, cut, local_cols)]
    last_cuts = [(0, cut), (cut, local_cols)]
    partner = row ^ jnp.arange(rows_n, dtype=jnp.int32)

    def columns(matrix, cuts):
        cube = matrix.reshape(matrix.shape[0], cols_n, local_cols)
        kept = [cube[:, :, lo:hi].reshape(matrix.shape[0], -1) for lo, hi in cuts]
        return jnp.concatenate(split(jnp.concatenate(kept, 1).T), 0)

    c_one = columns(coupling[0], [(0, local_cols)])
    c_two = columns(coupling[1], last_cuts)
    c_three = columns(coupling[2], last_cuts)

    def gather(shard):
        return lax.all_gather(shard, "pcol", axis=0, tiled=True)

    def send(pieces):
        return [exchange(p, "prow", rows_n, s + 1) for s, p in enumerate(pieces)]

    def to_columns(groups):
        return lax.all_to_all(negative_sums(order, groups, cols_n), "pcol", 0, 0)

    def to_rows(value):
        count = value.shape[1]
        value = value.reshape(rows_n, ratio * count, part)
        value = lax.all_to_all(value, "prow", 0, 0)
        return value.reshape(rows_n, ratio, count, part)

    def share(value):
        return [value] + [exchange(value, "prow", rows_n, s) for s in range(1, rows_n)]

    first, second, third = coupling[0], coupling[1], coupling[2]
    start = col * local_cols

    def own_rows(matrix):
        return lax.dynamic_slice_in_dim(matrix, start, local_cols, 0)

    def own_cols(matrix):
        return lax.dynamic_slice_in_dim(matrix, start, local_cols, 1)

    bridge = second - matmul(first, third)
    d0 = own_rows(dinv[0])
    d1 = own_rows(dinv[1])
    k0 = tdot(own_cols(first), dinv[0])
    k1 = tdot(own_cols(bridge), dinv[0])
    k2 = tdot(own_cols(third), dinv[1])
    base_cross = jnp.stack(
        [-matmul(d0, first), -matmul(d0, bridge), matmul(k0, bridge) - matmul(d1, third)], 0
    )
    base_diag = jnp.stack(
        [d0, d1 + matmul(k0, first), own_rows(dinv[2]) + matmul(k1, bridge) + matmul(k2, third)], 0
    )

    order = Order()
    shard = masked(order, turned, mask, *chunks[0], [])
    g0 = gather(shard)
    inverse = prepared(order, ainv, partner, rows_n, part)

    early_work = [c_one, c_two, c_three, base_cross, base_diag]
    early_work = [c_one, c_two, c_three, base_cross, base_diag]
    shard = masked(order, turned, mask, *chunks[1], [g0] + early_work)
    g1 = gather(shard)
    f0, sent = products(order, g0, inverse, 0, rows_n)
    s0 = [sent[0]] + send(sent[1:])
    pre1 = elimination(order, [(c_one, f0)], [cols_n * local_cols])
    m0 = to_columns([s0])

    shard = masked(order, turned, mask, *chunks[2], [g1])
    g2 = gather(shard)
    f1, sent = products(order, g1, inverse, 0, rows_n, pre1[0])
    s1 = [sent[0]] + send(sent[1:])
    m0 = to_rows(relay(order, m0))
    pre2 = elimination(
        order, [(c_two, f0), (c_three, f1)], [cols_n * (hi - lo) for lo, hi in last_cuts]
    )

    shard = masked(order, turned, mask, *chunks[3], [g2])
    g3 = gather(shard)
    f2, sent = products(order, g2, inverse, 0, rows_n, pre2[0])
    s2 = [sent[0]] + send(sent[1:])
    whole = assembled(order, m0, 0, turned.shape)
    m1 = to_columns([s1])

    f3, sent = products(order, g3, inverse, 1, rows_n, pre2[1])
    s3 = send(sent)
    _, own3 = products(order, f3, inverse, 0, 1)
    m2 = to_columns([s2])
    m3 = to_columns([own3 + s3])
    m1 = to_rows(relay(order, m1))
    columns_n = cols_n * local_cols
    begin = cols_n * cut
    last = [(0, 0), (0, begin)]
    one = inner_products(
        order, whole, 0, [f0, f1, f2, f3],
        [(0, 0), (local_cols, 0)] + [(2 * local_cols, c) for _, c in last],
        (3 * local_cols, columns_n),
    )
    one = share(one)
    m23 = to_rows(relay(order, m2, m3))
    whole = assembled(order, m1, 1, turned.shape, whole)
    two = inner_products(
        order, whole, 1, [f1, f2, f3], [(0, 0)] + [(local_cols, c) for _, c in last],
        (2 * local_cols, columns_n),
    )
    two = share(two)
    whole = assembled(order, m23, 2, turned.shape, whole)
    three = inner_products(
        order, whole, 2, [f2, f3], last, (local_cols, columns_n), one[1:]
    )
    three = share(three)
    cross, diag = finish(
        order, one, two, three, base_cross, base_diag, cols_n, (cut, local_cols - cut)
    )
    return (jnp.swapaxes(whole, 1, 2), cross, diag)


def solution(mesh):
    placed = (P("prow", "pcol"), P(None, "prow", "pcol"), P(), P(), P())
    return jax.shard_map(
        shards,
        mesh=mesh,
        in_specs=placed,
        out_specs=(P(None, "prow", "pcol"), P(None, "pcol", None), P(None, "pcol", None)),
        check_vma=False,
    )
```

```python
import functools

import jax
import jax.numpy as jnp
from jax import lax
from jax.experimental import pallas as pl
from jax.experimental.pallas import tpu as pltpu
from jax.sharding import PartitionSpec as P

NB = 128
MIB = 1024 * 1024

precise = lax.Precision.HIGHEST


def matmul(left, right):
    return jnp.dot(left, right, precision=precise, preferred_element_type=jnp.float32)


def tdot(left, right):
    return lax.dot_general(
        left, right, (((0,), (0,)), ((), ())), precision=precise, preferred_element_type=jnp.float32
    )


def tile_of(size, wanted):
    return wanted if size % wanted == 0 else size


def split(values):
    high = lax.reduce_precision(values, exponent_bits=8, mantissa_bits=7)
    return high.astype(jnp.bfloat16), (values - high).astype(jnp.bfloat16)


def split_here(values):
    high = values.astype(jnp.bfloat16)
    return high, (values - high.astype(jnp.float32)).astype(jnp.bfloat16)


def triple_dot(left, right_high, right_low, contract=(1, 0)):
    dims = (((contract[0],), (contract[1],)), ((), ()))
    rows = left.shape[0] // 2
    wide = lax.dot_general(left, right_high, dims, preferred_element_type=jnp.float32)
    cross = lax.dot_general(left[:rows], right_low, dims, preferred_element_type=jnp.float32)
    return wide[:rows] + wide[rows:] + cross


def exchange(value, axis, size, step):
    return lax.ppermute(value, axis, [(i, i ^ step) for i in range(size)])


class Order:
    def __init__(self):
        self.last = None

    def __call__(self, kernel, operands, in_specs, out_shape, out_specs, grid, flops, moved,
                 name, scratch=(), limit=56, prefetch=(), extra=(), aliases=None):
        tokens = list(extra) + ([] if self.last is None else [self.last])
        skip = len(prefetch) + len(operands)

        def body(*refs):
            kernel(*refs[:skip], *refs[skip + len(tokens):])

        got = pl.pallas_call(
            body,
            out_shape=out_shape,
            grid_spec=pltpu.PrefetchScalarGridSpec(
                num_scalar_prefetch=len(prefetch),
                grid=grid,
                in_specs=list(in_specs) + [pl.BlockSpec(memory_space=pl.ANY)] * len(tokens),
                out_specs=out_specs,
                scratch_shapes=list(scratch),
            ),
            compiler_params=pltpu.CompilerParams(vmem_limit_bytes=limit * MIB),
            cost_estimate=pl.CostEstimate(
                flops=flops // 16, bytes_accessed=moved // 16, transcendentals=0
            ),
            input_output_aliases=aliases or {},
            name=name,
        )(*prefetch, *operands, *tokens)
        self.last = got[0] if isinstance(got, (tuple, list)) else got
        return got


def shape_of(shape, dtype=jnp.float32):
    return jax.ShapeDtypeStruct(shape, dtype)


def mask_kernel(panel_ref, mask_ref, out_ref):
    out_ref[...] = panel_ref[0] * mask_ref[0]


def masked(order, panels, mask, j, lo, hi, extra):
    rows = panels.shape[2]
    count = hi - lo
    return order(
        mask_kernel,
        [panels, mask],
        [
            pl.BlockSpec((1, count, rows), lambda i: (j, lo // count, 0)),
            pl.BlockSpec((1, 1, rows), lambda i: (j, 0, 0)),
        ],
        shape_of((count, rows)),
        pl.BlockSpec((count, rows), lambda i: (0, 0)),
        (1,),
        count * rows,
        8 * count * rows,
        "masked",
        extra=extra,
    )


def prepare_kernel(partner_ref, a_ref, high_ref, low_ref):
    high_ref[0], low_ref[0] = split_here(a_ref[...])


def prepared(order, ainv, partner, count, part):
    rows = ainv.shape[0]
    if part % 128:
        pieces = [
            split(lax.dynamic_slice_in_dim(ainv, partner[s] * part, part, 1)) for s in range(count)
        ]
        return jnp.stack([p[0] for p in pieces], 0), jnp.stack([p[1] for p in pieces], 0)
    tile = tile_of(rows, 1024)
    shape = shape_of((count, rows, part), jnp.bfloat16)
    spec = pl.BlockSpec((1, tile, part), lambda s, i, partner: (s, i, 0))
    return order(
        prepare_kernel,
        [ainv],
        [pl.BlockSpec((tile, part), lambda s, i, partner: (i, partner[s]))],
        (shape, shape),
        (spec, spec),
        (count, rows // tile),
        4 * ainv.size,
        8 * ainv.size,
        "prepared",
        prefetch=[partner],
    )


def product_kernel(count, steps, with_pre, with_split, *refs):
    refs = list(refs)
    s, k = pl.program_id(0), pl.program_id(1)
    if with_split:
        gathered_ref = refs.pop(0)
        pre_ref = refs.pop(0) if with_pre else None
        a_high_ref, a_low_ref = refs.pop(0), refs.pop(0)
        factor_ref = refs.pop(0)
        outer, strip, depth = gathered_ref.shape
        rows = outer * strip
        here = pl.ds(pl.multiple_of(k * depth, depth), depth)

        @pl.when(s == 0)
        def _():
            @pl.loop(0, outer)
            def _(i):
                first = pl.multiple_of(i * strip, strip)
                values = gathered_ref[i]
                if with_pre:
                    values = values - pre_ref[pl.ds(first, strip), :]
                high, low = split_here(values)
                factor_ref[pl.ds(first, strip), here] = high
                factor_ref[pl.ds(pl.multiple_of(first + rows, strip), strip), here] = low

        factor = factor_ref[:, here]
    else:
        factor_ref, a_high_ref, a_low_ref = refs[:3]
        refs = refs[3:]
        factor = factor_ref[...]
    outs, total_ref = refs[:count], refs[count]
    value = triple_dot(factor, a_high_ref[0], a_low_ref[0])

    @pl.when(k == 0)
    def _():
        total_ref[...] = value

    @pl.when(k > 0)
    def _():
        total_ref[...] += value

    for i in range(count):
        @pl.when((s == i) & (k == steps - 1))
        def _():
            outs[i][...] = total_ref[...]


def products(order, factor, inverse, first, last, pre=None, piece=(0, 1)):
    with_split = factor.dtype == jnp.float32
    a_high, a_low = inverse
    count = last - first
    part = a_high.shape[2]
    length = factor.shape[-1]
    if with_split:
        strip = factor.shape[1] // piece[1]
        rows = factor.shape[0] * strip
    else:
        rows = factor.shape[0] // 2
    depth = tile_of(length, 2048)
    steps = length // depth
    a_spec = pl.BlockSpec((1, depth, part), lambda s, k: (s + first, k, 0))
    out_shape = [shape_of((rows, part))] * count
    out_specs = [pl.BlockSpec((rows, part), lambda s, k: (0, 0))] * count
    if with_split:
        operands = [factor] + ([] if pre is None else [pre]) + [a_high, a_low]

        def once(k, s):
            return jnp.where(s == 0, k, steps - 1)

        in_specs = [
            pl.BlockSpec((factor.shape[0], strip, depth), lambda s, k: (0, piece[0], once(k, s))),
            pl.BlockSpec((rows, depth), lambda s, k: (0, once(k, s))),
        ][: len(operands) - 2] + [a_spec, a_spec]
        out_shape = [shape_of((2 * rows, length), jnp.bfloat16)] + out_shape
        out_specs = [pl.BlockSpec((2 * rows, length), lambda s, k: (0, 0))] + out_specs
    else:
        operands = [factor, a_high, a_low]
        in_specs = [pl.BlockSpec((2 * rows, depth), lambda s, k: (0, k)), a_spec, a_spec]
    got = order(
        functools.partial(product_kernel, count, steps, pre is not None, with_split),
        operands,
        in_specs,
        out_shape,
        out_specs,
        (count, steps),
        6 * rows * length * part * count,
        4 * length * part * count + 8 * rows * length,
        "products",
        scratch=[pltpu.VMEM((rows, part), jnp.float32)],
    )
    if with_split:
        return got[0], list(got[1:])
    return factor, list(got)


def elimination_kernel(sources, sizes, *refs):
    value = None
    for i in range(sources):
        coupled, factor_ref = refs[2 * i][...], refs[2 * i + 1]
        depth = factor_ref.shape[0] // 2
        term = triple_dot(coupled, factor_ref[:depth, :], factor_ref[depth:, :])
        value = term if value is None else value + term
    start = 0
    for ref, size in zip(refs[2 * sources :], sizes):
        ref[...] = value[start : start + size]
        start += size


def elimination(order, pairs, sizes, extra=()):
    operands = [value for pair in pairs for value in pair]
    rows, depth = pairs[0][0].shape[0] // 2, pairs[0][0].shape[1]
    length = pairs[0][1].shape[1]
    tile = tile_of(length, 512)
    left = pl.BlockSpec((2 * rows, depth), lambda i: (0, 0))
    right = pl.BlockSpec((2 * depth, tile), lambda i: (0, i))
    return order(
        functools.partial(elimination_kernel, len(pairs), sizes),
        operands,
        [left, right] * len(pairs),
        [shape_of((size, length)) for size in sizes],
        [pl.BlockSpec((size, tile), lambda i: (0, i)) for size in sizes],
        (length // tile,),
        6 * rows * depth * length * len(pairs),
        4 * length * (rows + depth * len(pairs)),
        "elimination",
        extra=extra,
    )


def sum_kernel(shares, *refs):
    out = refs[-1]
    start = 0
    for i in range(0, len(refs) - 1, shares):
        value = refs[i][...]
        for ref in refs[i + 1 : i + shares]:
            value = value + ref[...]
        out[0, start : start + value.shape[0], :] = -value
        start += value.shape[0]


def negative_sums(order, groups, cols_n):
    flat = [value for group in groups for value in group]
    width = flat[0].shape[1]
    counts = [group[0].shape[0] // cols_n for group in groups]
    shape = (cols_n, sum(counts), width)
    return order(
        functools.partial(sum_kernel, len(groups[0])),
        flat,
        [pl.BlockSpec((v.shape[0] // cols_n, width), lambda i: (i, 0)) for v in flat],
        shape_of(shape),
        pl.BlockSpec((1, sum(counts), width), lambda i: (i, 0, 0)),
        (cols_n,),
        sum(v.size for v in flat),
        4 * sum(v.size for v in flat),
        "negative_sums",
    )


def relay_kernel(*refs):
    start = 0
    for ref in refs[:-1]:
        refs[-1][:, start : start + ref.shape[1], :] = ref[...]
        start += ref.shape[1]


def relay(order, *values):
    outer, _, width = values[0].shape
    counts = [v.shape[1] for v in values]
    half = outer // 2
    return order(
        relay_kernel,
        list(values),
        [pl.BlockSpec((half, n, width), lambda i: (i, 0, 0)) for n in counts],
        shape_of((outer, sum(counts), width)),
        pl.BlockSpec((half, sum(counts), width), lambda i: (i, 0, 0)),
        (2,),
        sum(v.size for v in values),
        8 * sum(v.size for v in values),
        "relay",
    )


def assembly_kernel(in_ref, *refs):
    out_ref = refs[-1]
    outer, inner, _, part = in_ref.shape
    count = out_ref.shape[1]
    for i in range(out_ref.shape[0]):
        for a in range(inner):
            for q in range(outer):
                to = pl.ds((a * outer + q) * part, part)
                out_ref[i, :, to] = in_ref[q, a, i * count : (i + 1) * count, :]


def assembled(order, value, j, n, shape, whole=None):
    operands = [value] + ([] if whole is None else [whole])
    return order(
        assembly_kernel,
        operands,
        [pl.BlockSpec(value.shape, lambda i: (0, 0, 0, 0))]
        + [pl.BlockSpec(memory_space=pl.ANY)] * (len(operands) - 1),
        shape_of(shape),
        pl.BlockSpec((n, *shape[1:]), lambda i: (j, 0, 0)),
        (1,),
        value.size,
        8 * value.size,
        "assembled",
        aliases={} if whole is None else {1: 0},
    )


def inner_kernel(terms, *refs):
    out = refs[-1]

    @pl.when(pl.program_id(0) == 0)
    def _():
        out[...] = jnp.zeros_like(out)

    left = refs[0][...]
    left = -left.reshape(left.shape[0] * left.shape[1], left.shape[2])
    stacked = jnp.concatenate(split_here(left), 0)
    for right, (row, column, kept) in zip(refs[1:-1], terms):
        half = right.shape[0] // 2
        value = triple_dot(stacked, right[:half], right[half:], (1, 1))
        out[row : row + kept, column : column + half] += value[:kept]


def inner_products(order, whole, j, n, rights, terms, shape, extra=()):
    _, count, length = whole.shape
    depth = tile_of(length, 1024)
    return order(
        functools.partial(inner_kernel, terms),
        [whole] + list(rights),
        [pl.BlockSpec((n, count, depth), lambda k: (j, 0, k))]
        + [pl.BlockSpec((v.shape[0], depth), lambda k: (0, k)) for v in rights],
        shape_of(shape),
        pl.BlockSpec(shape, lambda k: (0, 0)),
        (length // depth,),
        6 * shape[0] * shape[1] * length,
        sum(2 * v.size for v in rights),
        "inner_products",
        extra=extra,
    )


def finish_kernel(shares, cols_n, sizes, *refs):
    def total(first):
        value = refs[first][...]
        for ref in refs[first + 1 : first + shares]:
            value = value + ref[...]
        return value

    one, two = (total(shares * i) for i in range(2))
    base_cross, base_diag, cross, diag, place = refs[2 * shares :]
    wide = sum(sizes)
    cut = cols_n * sizes[0]
    place[: 2 * wide, :] = one[3 * wide :]
    place[2 * wide :, :] = two

    def put(out, base, i, row):
        for c in range(cols_n):
            for start, first, size in ((0, 0, sizes[0]), (sizes[0], cut, sizes[1])):
                to = pl.ds(c * wide + start, size)
                out[i, :, to] = base[i, :, to] + place[row : row + wide, pl.ds(first + c * size, size)]

    diag[0] = base_diag[0] + one[:wide]
    cross[0] = base_cross[0] + one[wide : 2 * wide]
    diag[1] = base_diag[1] + one[2 * wide : 3 * wide]
    put(cross, base_cross, 1, 0)
    put(cross, base_cross, 2, wide)
    put(diag, base_diag, 2, 2 * wide)


def finish(order, one, two, base_cross, base_diag, cols_n, sizes):
    operands = one + two + [base_cross, base_diag]
    shape = base_cross.shape
    once = [pl.BlockSpec(v.shape, lambda i, n=v.ndim: (0,) * n) for v in operands]
    moved = 4 * sum(v.size for v in operands)
    return order(
        functools.partial(finish_kernel, len(one), cols_n, sizes),
        operands,
        once,
        [shape_of(shape)] * 2,
        [once[-1]] * 2,
        (1,),
        moved // 4,
        moved,
        "finish",
        scratch=[pltpu.VMEM((3 * shape[1], shape[2]), jnp.float32)],
    )


def shards(ainv, panels, pattern, coupling, dinv):
    rows_n = lax.axis_size("prow")
    cols_n = lax.axis_size("pcol")
    row = lax.axis_index("prow")
    col = lax.axis_index("pcol")
    local_rows, local_cols = panels.shape[1:]
    part = ainv.shape[1] // rows_n
    ratio = cols_n // rows_n
    blocks_here = local_rows // NB

    flags = lax.dynamic_slice_in_dim(pattern, row * blocks_here, blocks_here, 1)
    mask = jnp.repeat(flags.astype(jnp.float32), NB, axis=1)[:, None, :]
    turned = jnp.swapaxes(panels, 1, 2)

    cut = local_cols // 2
    last_cuts = [(0, cut), (cut, local_cols)]
    partner = row ^ jnp.arange(rows_n, dtype=jnp.int32)

    def columns(matrix, cuts):
        cube = matrix.reshape(matrix.shape[0], cols_n, local_cols)
        kept = [cube[:, :, lo:hi].reshape(matrix.shape[0], -1) for lo, hi in cuts]
        return jnp.concatenate(split(jnp.concatenate(kept, 1).T), 0)

    c_one = columns(coupling[0], [(0, local_cols)])
    c_two = columns(coupling[1], last_cuts)
    c_three = columns(coupling[2], last_cuts)

    def gather(shard):
        return lax.all_gather(shard, "pcol", axis=0, tiled=True).reshape(cols_n, *shard.shape)

    def send(pieces):
        return [exchange(p, "prow", rows_n, s + 1) for s, p in enumerate(pieces)]

    def to_columns(groups):
        return lax.all_to_all(negative_sums(order, groups, cols_n), "pcol", 0, 0)

    def to_rows(value):
        count = value.shape[1]
        value = value.reshape(rows_n, ratio * count, part)
        value = lax.all_to_all(value, "prow", 0, 0)
        return value.reshape(rows_n, ratio, count, part)

    def share(value):
        return [value] + [exchange(value, "prow", rows_n, s) for s in range(1, rows_n)]

    first, second, third = coupling[0], coupling[1], coupling[2]
    start = col * local_cols

    def own_rows(matrix):
        return lax.dynamic_slice_in_dim(matrix, start, local_cols, 0)

    def own_cols(matrix):
        return lax.dynamic_slice_in_dim(matrix, start, local_cols, 1)

    bridge = second - matmul(first, third)
    d0 = own_rows(dinv[0])
    d1 = own_rows(dinv[1])
    k0 = tdot(own_cols(first), dinv[0])
    k1 = tdot(own_cols(bridge), dinv[0])
    k2 = tdot(own_cols(third), dinv[1])
    base_cross = jnp.stack(
        [-matmul(d0, first), -matmul(d0, bridge), matmul(k0, bridge) - matmul(d1, third)], 0
    )
    base_diag = jnp.stack(
        [d0, d1 + matmul(k0, first), own_rows(dinv[2]) + matmul(k1, bridge) + matmul(k2, third)], 0
    )

    order = Order()
    shard = masked(order, turned, mask, 0, 0, local_cols, [])
    g0 = gather(shard)
    inverse = prepared(order, ainv, partner, rows_n, part)

    early_work = [c_one, c_two, c_three, base_cross, base_diag]
    early_work = [c_one, c_two, c_three, base_cross, base_diag]
    early_work = [c_one, c_two, c_three, base_cross, base_diag]
    shard = masked(order, turned, mask, 1, 0, local_cols, [g0] + early_work)
    g1 = gather(shard)
    f0, sent = products(order, g0, inverse, 0, rows_n)
    s0 = [sent[0]] + send(sent[1:])
    pre1 = elimination(order, [(c_one, f0)], [cols_n * local_cols])

    shard = masked(order, turned, mask, 2, 0, local_cols, [g1])
    g2 = gather(shard)
    f1, sent = products(order, g1, inverse, 0, rows_n, pre1[0])
    s1 = [sent[0]] + send(sent[1:])
    pre2 = elimination(
        order, [(c_two, f0), (c_three, f1)], [cols_n * (hi - lo) for lo, hi in last_cuts], s0[1:]
    )
    m01 = to_columns([s0, s1])

    f2, sent = products(order, g2, inverse, 0, rows_n, pre2[0], (0, 2))
    s2 = [sent[0]] + send(sent[1:])
    f3, sent = products(order, g2, inverse, 1, rows_n, pre2[1], (1, 2))
    s3 = send(sent)
    m2 = to_columns([s2])
    _, own3 = products(order, f3, inverse, 0, 1)
    m01 = to_rows(relay(order, m01))
    m3 = to_columns([own3 + s3])
    whole = assembled(order, m01, 0, 2, turned.shape)
    m23 = to_rows(relay(order, m2, m3))
    columns_n, begin, pair = cols_n * local_cols, cols_n * cut, 2 * local_cols
    one = inner_products(
        order, whole, 0, 2, [f0, f1, f2, f3],
        [(0, 0, local_cols), (local_cols, 0, pair)]
        + [(local_cols + pair, c, pair) for c in (0, begin)],
        (local_cols + 2 * pair, columns_n),
    )
    one = share(one)
    whole = assembled(order, m23, 2, 1, turned.shape, whole)
    two = inner_products(
        order, whole, 2, 1, [f2, f3], [(0, c, local_cols) for c in (0, begin)],
        (local_cols, columns_n), one[1:],
    )
    two = share(two)
    cross, diag = finish(
        order, one, two, base_cross, base_diag, cols_n, (cut, local_cols - cut)
    )
    return (jnp.swapaxes(whole, 1, 2), cross, diag)


def solution(mesh):
    placed = (P("prow", "pcol"), P(None, "prow", "pcol"), P(), P(), P())
    return jax.shard_map(
        shards,
        mesh=mesh,
        in_specs=placed,
        out_specs=(P(None, "prow", "pcol"), P(None, "pcol", None), P(None, "pcol", None)),
        check_vma=False,
    )
```

```python
import functools

import jax
import jax.numpy as jnp
from jax import lax
from jax.experimental import pallas as pl
from jax.experimental.pallas import tpu as pltpu
from jax.sharding import PartitionSpec as P

NB = 128
MIB = 1024 * 1024

precise = lax.Precision.HIGHEST


def matmul(left, right):
    return jnp.dot(left, right, precision=precise, preferred_element_type=jnp.float32)


def tdot(left, right):
    return lax.dot_general(
        left, right, (((0,), (0,)), ((), ())), precision=precise, preferred_element_type=jnp.float32
    )


def tile_of(size, wanted):
    return wanted if size % wanted == 0 else size


def split(values):
    high = lax.reduce_precision(values, exponent_bits=8, mantissa_bits=7)
    return high.astype(jnp.bfloat16), (values - high).astype(jnp.bfloat16)


def split_here(values):
    high = values.astype(jnp.bfloat16)
    return high, (values - high.astype(jnp.float32)).astype(jnp.bfloat16)


def triple_dot(left, right_high, right_low, contract=(1, 0)):
    dims = (((contract[0],), (contract[1],)), ((), ()))
    rows = left.shape[0] // 2
    wide = lax.dot_general(left, right_high, dims, preferred_element_type=jnp.float32)
    cross = lax.dot_general(left[:rows], right_low, dims, preferred_element_type=jnp.float32)
    return wide[:rows] + wide[rows:] + cross


def exchange(value, axis, size, step):
    return lax.ppermute(value, axis, [(i, i ^ step) for i in range(size)])


class Order:
    def __init__(self):
        self.last = None

    def __call__(self, kernel, operands, in_specs, out_shape, out_specs, grid, flops, moved,
                 name, scratch=(), limit=56, prefetch=(), extra=(), aliases=None):
        tokens = list(extra) + ([] if self.last is None else [self.last])
        skip = len(prefetch) + len(operands)

        def body(*refs):
            kernel(*refs[:skip], *refs[skip + len(tokens):])

        got = pl.pallas_call(
            body,
            out_shape=out_shape,
            grid_spec=pltpu.PrefetchScalarGridSpec(
                num_scalar_prefetch=len(prefetch),
                grid=grid,
                in_specs=list(in_specs) + [pl.BlockSpec(memory_space=pl.ANY)] * len(tokens),
                out_specs=out_specs,
                scratch_shapes=list(scratch),
            ),
            compiler_params=pltpu.CompilerParams(vmem_limit_bytes=limit * MIB),
            cost_estimate=pl.CostEstimate(
                flops=flops // 16, bytes_accessed=moved // 16, transcendentals=0
            ),
            input_output_aliases=aliases or {},
            name=name,
        )(*prefetch, *operands, *tokens)
        self.last = got[0] if isinstance(got, (tuple, list)) else got
        return got


def shape_of(shape, dtype=jnp.float32):
    return jax.ShapeDtypeStruct(shape, dtype)


def mask_kernel(panel_ref, mask_ref, out_ref):
    out_ref[...] = panel_ref[0] * mask_ref[0]


def masked(order, panels, mask, j, lo, hi, extra):
    rows = panels.shape[2]
    count = hi - lo
    return order(
        mask_kernel,
        [panels, mask],
        [
            pl.BlockSpec((1, count, rows), lambda i: (j, lo // count, 0)),
            pl.BlockSpec((1, 1, rows), lambda i: (j, 0, 0)),
        ],
        shape_of((count, rows)),
        pl.BlockSpec((count, rows), lambda i: (0, 0)),
        (1,),
        count * rows,
        8 * count * rows,
        "masked",
        extra=extra,
    )


def prepare_kernel(partner_ref, a_ref, high_ref, low_ref):
    high_ref[0], low_ref[0] = split_here(a_ref[...])


def prepared(order, ainv, partner, count, part):
    rows = ainv.shape[0]
    if part % 128:
        pieces = [
            split(lax.dynamic_slice_in_dim(ainv, partner[s] * part, part, 1)) for s in range(count)
        ]
        return jnp.stack([p[0] for p in pieces], 0), jnp.stack([p[1] for p in pieces], 0)
    tile = tile_of(rows, 1024)
    shape = shape_of((count, rows, part), jnp.bfloat16)
    spec = pl.BlockSpec((1, tile, part), lambda s, i, partner: (s, i, 0))
    return order(
        prepare_kernel,
        [ainv],
        [pl.BlockSpec((tile, part), lambda s, i, partner: (i, partner[s]))],
        (shape, shape),
        (spec, spec),
        (count, rows // tile),
        4 * ainv.size,
        8 * ainv.size,
        "prepared",
        prefetch=[partner],
    )


def product_kernel(count, steps, with_pre, with_split, *refs):
    refs = list(refs)
    s, k = pl.program_id(0), pl.program_id(1)
    if with_split:
        gathered_ref = refs.pop(0)
        pre_ref = refs.pop(0) if with_pre else None
        a_high_ref, a_low_ref = refs.pop(0), refs.pop(0)
        factor_ref = refs.pop(0)
        outer, strip, depth = gathered_ref.shape
        rows = outer * strip
        here = pl.ds(pl.multiple_of(k * depth, depth), depth)

        @pl.when(s == 0)
        def _():
            @pl.loop(0, outer)
            def _(i):
                first = pl.multiple_of(i * strip, strip)
                values = gathered_ref[i]
                if with_pre:
                    values = values - pre_ref[pl.ds(first, strip), :]
                high, low = split_here(values)
                factor_ref[pl.ds(first, strip), here] = high
                factor_ref[pl.ds(pl.multiple_of(first + rows, strip), strip), here] = low

        factor = factor_ref[:, here]
    else:
        factor_ref, a_high_ref, a_low_ref = refs[:3]
        refs = refs[3:]
        factor = factor_ref[...]
    outs, total_ref = refs[:count], refs[count]
    value = triple_dot(factor, a_high_ref[0], a_low_ref[0])

    @pl.when(k == 0)
    def _():
        total_ref[...] = value

    @pl.when(k > 0)
    def _():
        total_ref[...] += value

    for i in range(count):
        @pl.when((s == i) & (k == steps - 1))
        def _():
            outs[i][...] = total_ref[...]


def products(order, factor, inverse, first, last, pre=None, piece=(0, 1)):
    with_split = factor.dtype == jnp.float32
    a_high, a_low = inverse
    count = last - first
    part = a_high.shape[2]
    length = factor.shape[-1]
    if with_split:
        strip = factor.shape[1] // piece[1]
        rows = factor.shape[0] * strip
    else:
        rows = factor.shape[0] // 2
    depth = tile_of(length, 2048)
    steps = length // depth
    a_spec = pl.BlockSpec((1, depth, part), lambda s, k: (s + first, k, 0))
    out_shape = [shape_of((rows, part))] * count
    out_specs = [pl.BlockSpec((rows, part), lambda s, k: (0, 0))] * count
    if with_split:
        operands = [factor] + ([] if pre is None else [pre]) + [a_high, a_low]

        def once(k, s):
            return jnp.where(s == 0, k, steps - 1)

        in_specs = [
            pl.BlockSpec((factor.shape[0], strip, depth), lambda s, k: (0, piece[0], once(k, s))),
            pl.BlockSpec((rows, depth), lambda s, k: (0, once(k, s))),
        ][: len(operands) - 2] + [a_spec, a_spec]
        out_shape = [shape_of((2 * rows, length), jnp.bfloat16)] + out_shape
        out_specs = [pl.BlockSpec((2 * rows, length), lambda s, k: (0, 0))] + out_specs
    else:
        operands = [factor, a_high, a_low]
        in_specs = [pl.BlockSpec((2 * rows, depth), lambda s, k: (0, k)), a_spec, a_spec]
    got = order(
        functools.partial(product_kernel, count, steps, pre is not None, with_split),
        operands,
        in_specs,
        out_shape,
        out_specs,
        (count, steps),
        6 * rows * length * part * count,
        4 * length * part * count + 8 * rows * length,
        "products",
        scratch=[pltpu.VMEM((rows, part), jnp.float32)],
    )
    if with_split:
        return got[0], list(got[1:])
    return factor, list(got)


def elimination_kernel(sources, sizes, *refs):
    value = None
    for i in range(sources):
        coupled, factor_ref = refs[2 * i][...], refs[2 * i + 1]
        depth = factor_ref.shape[0] // 2
        term = triple_dot(coupled, factor_ref[:depth, :], factor_ref[depth:, :])
        value = term if value is None else value + term
    start = 0
    for ref, size in zip(refs[2 * sources :], sizes):
        ref[...] = value[start : start + size]
        start += size


def elimination(order, pairs, sizes, extra=()):
    operands = [value for pair in pairs for value in pair]
    rows, depth = pairs[0][0].shape[0] // 2, pairs[0][0].shape[1]
    length = pairs[0][1].shape[1]
    tile = tile_of(length, 512)
    left = pl.BlockSpec((2 * rows, depth), lambda i: (0, 0))
    right = pl.BlockSpec((2 * depth, tile), lambda i: (0, i))
    return order(
        functools.partial(elimination_kernel, len(pairs), sizes),
        operands,
        [left, right] * len(pairs),
        [shape_of((size, length)) for size in sizes],
        [pl.BlockSpec((size, tile), lambda i: (0, i)) for size in sizes],
        (length // tile,),
        6 * rows * depth * length * len(pairs),
        4 * length * (rows + depth * len(pairs)),
        "elimination",
        extra=extra,
    )


def sum_kernel(shares, *refs):
    out = refs[-1]
    start = 0
    for i in range(0, len(refs) - 1, shares):
        value = refs[i][...]
        for ref in refs[i + 1 : i + shares]:
            value = value + ref[...]
        out[0, start : start + value.shape[0], :] = -value
        start += value.shape[0]


def negative_sums(order, groups, cols_n):
    flat = [value for group in groups for value in group]
    width = flat[0].shape[1]
    counts = [group[0].shape[0] // cols_n for group in groups]
    shape = (cols_n, sum(counts), width)
    return order(
        functools.partial(sum_kernel, len(groups[0])),
        flat,
        [pl.BlockSpec((v.shape[0] // cols_n, width), lambda i: (i, 0)) for v in flat],
        shape_of(shape),
        pl.BlockSpec((1, sum(counts), width), lambda i: (i, 0, 0)),
        (cols_n,),
        sum(v.size for v in flat),
        4 * sum(v.size for v in flat),
        "negative_sums",
    )


def relay_kernel(*refs):
    start = 0
    for ref in refs[:-1]:
        refs[-1][:, start : start + ref.shape[1], :] = ref[...]
        start += ref.shape[1]


def relay(order, *values):
    outer, _, width = values[0].shape
    counts = [v.shape[1] for v in values]
    half = outer // 2
    return order(
        relay_kernel,
        list(values),
        [pl.BlockSpec((half, n, width), lambda i: (i, 0, 0)) for n in counts],
        shape_of((outer, sum(counts), width)),
        pl.BlockSpec((half, sum(counts), width), lambda i: (i, 0, 0)),
        (2,),
        sum(v.size for v in values),
        8 * sum(v.size for v in values),
        "relay",
    )


def assembly_kernel(in_ref, *refs):
    out_ref = refs[-1]
    outer, inner, _, part = in_ref.shape
    count = out_ref.shape[1]
    for i in range(out_ref.shape[0]):
        for a in range(inner):
            for q in range(outer):
                to = pl.ds((a * outer + q) * part, part)
                out_ref[i, :, to] = in_ref[q, a, i * count : (i + 1) * count, :]


def assembled(order, value, j, n, shape, whole=None):
    operands = [value] + ([] if whole is None else [whole])
    return order(
        assembly_kernel,
        operands,
        [pl.BlockSpec(value.shape, lambda i: (0, 0, 0, 0))]
        + [pl.BlockSpec(memory_space=pl.ANY)] * (len(operands) - 1),
        shape_of(shape),
        pl.BlockSpec((n, *shape[1:]), lambda i: (j, 0, 0)),
        (1,),
        value.size,
        8 * value.size,
        "assembled",
        aliases={} if whole is None else {1: 0},
    )


def inner_kernel(terms, *refs):
    out = refs[-1]

    @pl.when(pl.program_id(0) == 0)
    def _():
        out[...] = jnp.zeros_like(out)

    left = refs[0][...]
    left = -left.reshape(left.shape[0] * left.shape[1], left.shape[2])
    stacked = jnp.concatenate(split_here(left), 0)
    for right, (row, column, kept) in zip(refs[1:-1], terms):
        half = right.shape[0] // 2
        value = triple_dot(stacked, right[:half], right[half:], (1, 1))
        out[row : row + kept, column : column + half] += value[:kept]


def inner_products(order, whole, j, n, rights, terms, shape, extra=()):
    _, count, length = whole.shape
    depth = tile_of(length, 1024)
    return order(
        functools.partial(inner_kernel, terms),
        [whole] + list(rights),
        [pl.BlockSpec((n, count, depth), lambda k: (j, 0, k))]
        + [pl.BlockSpec((v.shape[0], depth), lambda k: (0, k)) for v in rights],
        shape_of(shape),
        pl.BlockSpec(shape, lambda k: (0, 0)),
        (length // depth,),
        6 * shape[0] * shape[1] * length,
        sum(2 * v.size for v in rights),
        "inner_products",
        extra=extra,
    )


def finish_kernel(shares, cols_n, sizes, *refs):
    def total(first):
        value = refs[first][...]
        for ref in refs[first + 1 : first + shares]:
            value = value + ref[...]
        return value

    one, two = -refs[0][...], total(1)
    base_cross, base_diag, cross, diag, place = refs[1 + shares :]
    wide = sum(sizes)
    cut = cols_n * sizes[0]
    place[: 2 * wide, :] = one[3 * wide :]
    place[2 * wide :, :] = two

    def put(out, base, i, row):
        for c in range(cols_n):
            for start, first, size in ((0, 0, sizes[0]), (sizes[0], cut, sizes[1])):
                to = pl.ds(c * wide + start, size)
                out[i, :, to] = base[i, :, to] + place[row : row + wide, pl.ds(first + c * size, size)]

    diag[0] = base_diag[0] + one[:wide]
    cross[0] = base_cross[0] + one[wide : 2 * wide]
    diag[1] = base_diag[1] + one[2 * wide : 3 * wide]
    put(cross, base_cross, 1, 0)
    put(cross, base_cross, 2, wide)
    put(diag, base_diag, 2, 2 * wide)


def finish(order, one, two, base_cross, base_diag, cols_n, sizes):
    operands = [one] + two + [base_cross, base_diag]
    shape = base_cross.shape
    once = [pl.BlockSpec(v.shape, lambda i, n=v.ndim: (0,) * n) for v in operands]
    moved = 4 * sum(v.size for v in operands)
    return order(
        functools.partial(finish_kernel, len(two), cols_n, sizes),
        operands,
        once,
        [shape_of(shape)] * 2,
        [once[-1]] * 2,
        (1,),
        moved // 4,
        moved,
        "finish",
        scratch=[pltpu.VMEM((3 * shape[1], shape[2]), jnp.float32)],
    )


def shards(ainv, panels, pattern, coupling, dinv):
    rows_n = lax.axis_size("prow")
    cols_n = lax.axis_size("pcol")
    row = lax.axis_index("prow")
    col = lax.axis_index("pcol")
    local_rows, local_cols = panels.shape[1:]
    part = ainv.shape[1] // rows_n
    ratio = cols_n // rows_n
    blocks_here = local_rows // NB

    flags = lax.dynamic_slice_in_dim(pattern, row * blocks_here, blocks_here, 1)
    mask = jnp.repeat(flags.astype(jnp.float32), NB, axis=1)[:, None, :]
    turned = jnp.swapaxes(panels, 1, 2)

    cut = local_cols // 2
    last_cuts = [(0, cut), (cut, local_cols)]
    partner = row ^ jnp.arange(rows_n, dtype=jnp.int32)

    def columns(matrix, cuts):
        cube = matrix.reshape(matrix.shape[0], cols_n, local_cols)
        kept = [cube[:, :, lo:hi].reshape(matrix.shape[0], -1) for lo, hi in cuts]
        return jnp.concatenate(split(jnp.concatenate(kept, 1).T), 0)

    c_one = columns(coupling[0], [(0, local_cols)])
    c_two = columns(coupling[1], last_cuts)
    c_three = columns(coupling[2], last_cuts)

    def gather(shard):
        return lax.all_gather(shard, "pcol", axis=0, tiled=True).reshape(cols_n, *shard.shape)

    def send(pieces):
        return [exchange(p, "prow", rows_n, s + 1) for s, p in enumerate(pieces)]

    def to_columns(groups):
        return lax.all_to_all(negative_sums(order, groups, cols_n), "pcol", 0, 0)

    def to_rows(value):
        count = value.shape[1]
        value = value.reshape(rows_n, ratio * count, part)
        value = lax.all_to_all(value, "prow", 0, 0)
        return value.reshape(rows_n, ratio, count, part)

    def share(value):
        return [value] + [exchange(value, "prow", rows_n, s) for s in range(1, rows_n)]

    first, second, third = coupling[0], coupling[1], coupling[2]
    start = col * local_cols

    def own_rows(matrix):
        return lax.dynamic_slice_in_dim(matrix, start, local_cols, 0)

    def own_cols(matrix):
        return lax.dynamic_slice_in_dim(matrix, start, local_cols, 1)

    bridge = second - matmul(first, third)
    d0 = own_rows(dinv[0])
    d1 = own_rows(dinv[1])
    k0 = tdot(own_cols(first), dinv[0])
    k1 = tdot(own_cols(bridge), dinv[0])
    k2 = tdot(own_cols(third), dinv[1])
    base_cross = jnp.stack(
        [-matmul(d0, first), -matmul(d0, bridge), matmul(k0, bridge) - matmul(d1, third)], 0
    )
    base_diag = jnp.stack(
        [d0, d1 + matmul(k0, first), own_rows(dinv[2]) + matmul(k1, bridge) + matmul(k2, third)], 0
    )

    order = Order()
    shard = masked(order, turned, mask, 0, 0, local_cols, [])
    g0 = gather(shard)
    inverse = prepared(order, ainv, partner, rows_n, part)

    early_work = [c_one, c_two, c_three, base_cross, base_diag]
    early_work = [c_one, c_two, c_three, base_cross, base_diag]
    early_work = [c_one, c_two, c_three, base_cross, base_diag]
    shard = masked(order, turned, mask, 1, 0, local_cols, [g0] + early_work)
    g1 = gather(shard)
    f0, sent = products(order, g0, inverse, 0, rows_n)
    s0 = [sent[0]] + send(sent[1:])
    pre1 = elimination(order, [(c_one, f0)], [cols_n * local_cols])

    shard = masked(order, turned, mask, 2, 0, local_cols, [g1])
    g2 = gather(shard)
    f1, sent = products(order, g1, inverse, 0, rows_n, pre1[0])
    s1 = [sent[0]] + send(sent[1:])
    pre2 = elimination(
        order, [(c_two, f0), (c_three, f1)], [cols_n * (hi - lo) for lo, hi in last_cuts]
    )

    f2, sent = products(order, g2, inverse, 0, rows_n, pre2[0], (0, 2))
    s2 = [sent[0]] + send(sent[1:])
    m01 = to_columns([s0, s1])
    f3, sent = products(order, g2, inverse, 1, rows_n, pre2[1], (1, 2))
    s3 = send(sent)
    m2 = to_columns([s2])
    _, own3 = products(order, f3, inverse, 0, 1)
    m3 = to_columns([own3 + s3])
    m01 = to_rows(relay(order, m01))
    m23 = to_rows(relay(order, m2, m3))
    whole = assembled(order, m01, 0, 2, turned.shape)
    columns_n, begin, pair = cols_n * local_cols, cols_n * cut, 2 * local_cols
    one = inner_products(
        order, whole, 0, 2, [f0, f1, f2, f3],
        [(0, 0, local_cols), (local_cols, 0, pair)]
        + [(local_cols + pair, c, pair) for c in (0, begin)],
        (local_cols + 2 * pair, columns_n),
    )
    one = share(one)
    whole = assembled(order, m23, 2, 1, turned.shape, whole)
    two = inner_products(
        order, whole, 2, 1, [f2, f3], [(0, c, local_cols) for c in (0, begin)],
        (local_cols, columns_n),
    )
    two = share(two)
    one = negative_sums(order, [one], 1)[0]
    cross, diag = finish(
        order, one, two, base_cross, base_diag, cols_n, (cut, local_cols - cut)
    )
    return (jnp.swapaxes(whole, 1, 2), cross, diag)


def solution(mesh):
    placed = (P("prow", "pcol"), P(None, "prow", "pcol"), P(), P(), P())
    return jax.shard_map(
        shards,
        mesh=mesh,
        in_specs=placed,
        out_specs=(P(None, "prow", "pcol"), P(None, "pcol", None), P(None, "pcol", None)),
        check_vma=False,
    )
```

```python
import functools

import jax
import jax.numpy as jnp
from jax import lax
from jax.experimental import pallas as pl
from jax.experimental.pallas import tpu as pltpu
from jax.sharding import PartitionSpec as P

NB = 128
MIB = 1024 * 1024

precise = lax.Precision.HIGHEST


def matmul(left, right):
    return jnp.dot(left, right, precision=precise, preferred_element_type=jnp.float32)


def tdot(left, right):
    return lax.dot_general(
        left, right, (((0,), (0,)), ((), ())), precision=precise, preferred_element_type=jnp.float32
    )


def tile_of(size, wanted):
    return wanted if size % wanted == 0 else size


def split(values):
    high = lax.reduce_precision(values, exponent_bits=8, mantissa_bits=7)
    return high.astype(jnp.bfloat16), (values - high).astype(jnp.bfloat16)


def split_here(values):
    high = values.astype(jnp.bfloat16)
    return high, (values - high.astype(jnp.float32)).astype(jnp.bfloat16)


def triple_dot(left, right_high, right_low, contract=(1, 0)):
    dims = (((contract[0],), (contract[1],)), ((), ()))
    rows = left.shape[0] // 2
    wide = lax.dot_general(left, right_high, dims, preferred_element_type=jnp.float32)
    cross = lax.dot_general(left[:rows], right_low, dims, preferred_element_type=jnp.float32)
    return wide[:rows] + wide[rows:] + cross


def exchange(value, axis, size, step):
    return lax.ppermute(value, axis, [(i, i ^ step) for i in range(size)])


class Order:
    def __init__(self):
        self.last = None

    def __call__(self, kernel, operands, in_specs, out_shape, out_specs, grid, flops, moved,
                 name, scratch=(), limit=56, prefetch=(), extra=(), aliases=None):
        tokens = list(extra) + ([] if self.last is None else [self.last])
        skip = len(prefetch) + len(operands)

        def body(*refs):
            kernel(*refs[:skip], *refs[skip + len(tokens):])

        got = pl.pallas_call(
            body,
            out_shape=out_shape,
            grid_spec=pltpu.PrefetchScalarGridSpec(
                num_scalar_prefetch=len(prefetch),
                grid=grid,
                in_specs=list(in_specs) + [pl.BlockSpec(memory_space=pl.ANY)] * len(tokens),
                out_specs=out_specs,
                scratch_shapes=list(scratch),
            ),
            compiler_params=pltpu.CompilerParams(vmem_limit_bytes=limit * MIB),
            cost_estimate=pl.CostEstimate(
                flops=flops // 16, bytes_accessed=moved // 16, transcendentals=0
            ),
            input_output_aliases=aliases or {},
            name=name,
        )(*prefetch, *operands, *tokens)
        self.last = got[0] if isinstance(got, (tuple, list)) else got
        return got


def shape_of(shape, dtype=jnp.float32):
    return jax.ShapeDtypeStruct(shape, dtype)


def mask_kernel(panel_ref, mask_ref, out_ref):
    out_ref[...] = panel_ref[0] * mask_ref[0]


def masked(order, panels, mask, j, lo, hi, extra):
    rows = panels.shape[2]
    count = hi - lo
    return order(
        mask_kernel,
        [panels, mask],
        [
            pl.BlockSpec((1, count, rows), lambda i: (j, lo // count, 0)),
            pl.BlockSpec((1, 1, rows), lambda i: (j, 0, 0)),
        ],
        shape_of((count, rows)),
        pl.BlockSpec((count, rows), lambda i: (0, 0)),
        (1,),
        count * rows,
        8 * count * rows,
        "masked",
        extra=extra,
    )


def prepare_kernel(partner_ref, a_ref, high_ref, low_ref):
    high_ref[0], low_ref[0] = split_here(a_ref[...])


def prepared(order, ainv, partner, count, part):
    rows = ainv.shape[0]
    if part % 128:
        pieces = [
            split(lax.dynamic_slice_in_dim(ainv, partner[s] * part, part, 1)) for s in range(count)
        ]
        return jnp.stack([p[0] for p in pieces], 0), jnp.stack([p[1] for p in pieces], 0)
    tile = tile_of(rows, 1024)
    shape = shape_of((count, rows, part), jnp.bfloat16)
    spec = pl.BlockSpec((1, tile, part), lambda s, i, partner: (s, i, 0))
    return order(
        prepare_kernel,
        [ainv],
        [pl.BlockSpec((tile, part), lambda s, i, partner: (i, partner[s]))],
        (shape, shape),
        (spec, spec),
        (count, rows // tile),
        4 * ainv.size,
        8 * ainv.size,
        "prepared",
        prefetch=[partner],
    )


def product_kernel(count, steps, with_pre, with_split, *refs):
    refs = list(refs)
    s, k = pl.program_id(0), pl.program_id(1)
    if with_split:
        gathered_ref = refs.pop(0)
        pre_ref = refs.pop(0) if with_pre else None
        a_high_ref, a_low_ref = refs.pop(0), refs.pop(0)
        factor_ref = refs.pop(0)
        outer, strip, depth = gathered_ref.shape
        rows = outer * strip
        here = pl.ds(pl.multiple_of(k * depth, depth), depth)

        @pl.when(s == 0)
        def _():
            @pl.loop(0, outer)
            def _(i):
                first = pl.multiple_of(i * strip, strip)
                values = gathered_ref[i]
                if with_pre:
                    values = values - pre_ref[pl.ds(first, strip), :]
                high, low = split_here(values)
                factor_ref[pl.ds(first, strip), here] = high
                factor_ref[pl.ds(pl.multiple_of(first + rows, strip), strip), here] = low

        factor = factor_ref[:, here]
    else:
        factor_ref, a_high_ref, a_low_ref = refs[:3]
        refs = refs[3:]
        factor = factor_ref[...]
    outs, total_ref = refs[:count], refs[count]
    value = triple_dot(factor, a_high_ref[0], a_low_ref[0])

    @pl.when(k == 0)
    def _():
        total_ref[...] = value

    @pl.when(k > 0)
    def _():
        total_ref[...] += value

    for i in range(count):
        @pl.when((s == i) & (k == steps - 1))
        def _():
            outs[i][...] = total_ref[...]


def products(order, factor, inverse, first, last, pre=None, piece=(0, 1), extra=()):
    with_split = factor.dtype == jnp.float32
    a_high, a_low = inverse
    count = last - first
    part = a_high.shape[2]
    length = factor.shape[-1]
    if with_split:
        strip = factor.shape[1] // piece[1]
        rows = factor.shape[0] * strip
    else:
        rows = factor.shape[0] // 2
    depth = tile_of(length, 2048)
    steps = length // depth
    a_spec = pl.BlockSpec((1, depth, part), lambda s, k: (s + first, k, 0))
    out_shape = [shape_of((rows, part))] * count
    out_specs = [pl.BlockSpec((rows, part), lambda s, k: (0, 0))] * count
    if with_split:
        operands = [factor] + ([] if pre is None else [pre]) + [a_high, a_low]

        def once(k, s):
            return jnp.where(s == 0, k, steps - 1)

        in_specs = [
            pl.BlockSpec((factor.shape[0], strip, depth), lambda s, k: (0, piece[0], once(k, s))),
            pl.BlockSpec((rows, depth), lambda s, k: (0, once(k, s))),
        ][: len(operands) - 2] + [a_spec, a_spec]
        out_shape = [shape_of((2 * rows, length), jnp.bfloat16)] + out_shape
        out_specs = [pl.BlockSpec((2 * rows, length), lambda s, k: (0, 0))] + out_specs
    else:
        operands = [factor, a_high, a_low]
        in_specs = [pl.BlockSpec((2 * rows, depth), lambda s, k: (0, k)), a_spec, a_spec]
    got = order(
        functools.partial(product_kernel, count, steps, pre is not None, with_split),
        operands,
        in_specs,
        out_shape,
        out_specs,
        (count, steps),
        6 * rows * length * part * count,
        4 * length * part * count + 8 * rows * length,
        "products",
        scratch=[pltpu.VMEM((rows, part), jnp.float32)],
        extra=extra,
    )
    if with_split:
        return got[0], list(got[1:])
    return factor, list(got)


def elimination_kernel(sources, sizes, *refs):
    value = None
    for i in range(sources):
        coupled, factor_ref = refs[2 * i][...], refs[2 * i + 1]
        depth = factor_ref.shape[0] // 2
        term = triple_dot(coupled, factor_ref[:depth, :], factor_ref[depth:, :])
        value = term if value is None else value + term
    start = 0
    for ref, size in zip(refs[2 * sources :], sizes):
        ref[...] = value[start : start + size]
        start += size


def elimination(order, pairs, sizes, extra=()):
    operands = [value for pair in pairs for value in pair]
    rows, depth = pairs[0][0].shape[0] // 2, pairs[0][0].shape[1]
    length = pairs[0][1].shape[1]
    tile = tile_of(length, 512)
    left = pl.BlockSpec((2 * rows, depth), lambda i: (0, 0))
    right = pl.BlockSpec((2 * depth, tile), lambda i: (0, i))
    return order(
        functools.partial(elimination_kernel, len(pairs), sizes),
        operands,
        [left, right] * len(pairs),
        [shape_of((size, length)) for size in sizes],
        [pl.BlockSpec((size, tile), lambda i: (0, i)) for size in sizes],
        (length // tile,),
        6 * rows * depth * length * len(pairs),
        4 * length * (rows + depth * len(pairs)),
        "elimination",
        extra=extra,
    )


def sum_kernel(shares, *refs):
    out = refs[-1]
    start = 0
    for i in range(0, len(refs) - 1, shares):
        value = refs[i][...]
        for ref in refs[i + 1 : i + shares]:
            value = value + ref[...]
        out[0, start : start + value.shape[0], :] = -value
        start += value.shape[0]


def negative_sums(order, groups, cols_n):
    flat = [value for group in groups for value in group]
    width = flat[0].shape[1]
    counts = [group[0].shape[0] // cols_n for group in groups]
    shape = (cols_n, sum(counts), width)
    return order(
        functools.partial(sum_kernel, len(groups[0])),
        flat,
        [pl.BlockSpec((v.shape[0] // cols_n, width), lambda i: (i, 0)) for v in flat],
        shape_of(shape),
        pl.BlockSpec((1, sum(counts), width), lambda i: (i, 0, 0)),
        (cols_n,),
        sum(v.size for v in flat),
        4 * sum(v.size for v in flat),
        "negative_sums",
    )


def relay_kernel(count, partner_ref, *refs):
    outs = refs[count:]
    ratio = outs[0].shape[0]
    for s, out in enumerate(outs):
        first = partner_ref[s] * ratio
        for a in range(ratio):
            start = 0
            for ref in refs[:count]:
                out[a, start : start + ref.shape[1], :] = ref[first + a]
                start += ref.shape[1]


def relay(order, partner, values):
    outer, _, width = values[0].shape
    pieces = partner.shape[0]
    shape = (outer // pieces, sum(v.shape[1] for v in values), width)
    return order(
        functools.partial(relay_kernel, len(values)),
        list(values),
        [pl.BlockSpec(v.shape, lambda i, p: (0, 0, 0)) for v in values],
        [shape_of(shape)] * pieces,
        [pl.BlockSpec(shape, lambda i, p: (0, 0, 0))] * pieces,
        (1,),
        sum(v.size for v in values),
        8 * sum(v.size for v in values),
        "relay",
        prefetch=[partner],
    )


def assembly_kernel(count, partner_ref, *refs):
    out_ref = refs[-1]
    ratio, _, part = refs[0].shape
    for s in range(count):
        for q in range(count):

            @pl.when(partner_ref[s] == q)
            def _():
                for a in range(ratio):
                    out_ref[0, :, pl.ds((a * count + q) * part, part)] = refs[s][a]


def assembled(order, partner, values, j, shape, whole=None):
    count = len(values)
    operands = list(values) + ([] if whole is None else [whole])
    size = count * values[0].size
    return order(
        functools.partial(assembly_kernel, count),
        operands,
        [pl.BlockSpec(v.shape, lambda i, p: (0, 0, 0)) for v in values]
        + [pl.BlockSpec(memory_space=pl.ANY)] * (len(operands) - count),
        shape_of(shape),
        pl.BlockSpec((1, *shape[1:]), lambda i, p: (j, 0, 0)),
        (1,),
        size,
        8 * size,
        "assembled",
        prefetch=[partner],
        aliases={} if whole is None else {1 + count: 0},
    )


def inner_kernel(terms, *refs):
    out = refs[-1]

    @pl.when(pl.program_id(0) == 0)
    def _():
        out[...] = jnp.zeros_like(out)

    left = refs[0][...]
    left = -left.reshape(left.shape[0] * left.shape[1], left.shape[2])
    stacked = jnp.concatenate(split_here(left), 0)
    for right, (row, column, kept) in zip(refs[1:-1], terms):
        half = right.shape[0] // 2
        value = triple_dot(stacked, right[:half], right[half:], (1, 1))
        out[row : row + kept, column : column + half] += value[:kept]


def inner_products(order, whole, j, n, rights, terms, shape, extra=()):
    _, count, length = whole.shape
    depth = tile_of(length, 1024)
    return order(
        functools.partial(inner_kernel, terms),
        [whole] + list(rights),
        [pl.BlockSpec((n, count, depth), lambda k: (j, 0, k))]
        + [pl.BlockSpec((v.shape[0], depth), lambda k: (0, k)) for v in rights],
        shape_of(shape),
        pl.BlockSpec(shape, lambda k: (0, 0)),
        (length // depth,),
        6 * shape[0] * shape[1] * length,
        sum(2 * v.size for v in rights),
        "inner_products",
        extra=extra,
    )


def finish_kernel(shares, cols_n, sizes, *refs):
    def total(first):
        value = refs[first][...]
        for ref in refs[first + 1 : first + shares]:
            value = value + ref[...]
        return value

    one, two = -refs[0][...], total(1)
    base_cross, base_diag, cross, diag, place = refs[1 + shares :]
    wide = sum(sizes)
    cut = cols_n * sizes[0]
    place[: 2 * wide, :] = one[3 * wide :]
    place[2 * wide :, :] = two

    def put(out, base, i, row):
        for c in range(cols_n):
            for start, first, size in ((0, 0, sizes[0]), (sizes[0], cut, sizes[1])):
                to = pl.ds(c * wide + start, size)
                out[i, :, to] = base[i, :, to] + place[row : row + wide, pl.ds(first + c * size, size)]

    diag[0] = base_diag[0] + one[:wide]
    cross[0] = base_cross[0] + one[wide : 2 * wide]
    diag[1] = base_diag[1] + one[2 * wide : 3 * wide]
    put(cross, base_cross, 1, 0)
    put(cross, base_cross, 2, wide)
    put(diag, base_diag, 2, 2 * wide)


def finish(order, one, two, base_cross, base_diag, cols_n, sizes):
    operands = [one] + two + [base_cross, base_diag]
    shape = base_cross.shape
    once = [pl.BlockSpec(v.shape, lambda i, n=v.ndim: (0,) * n) for v in operands]
    moved = 4 * sum(v.size for v in operands)
    return order(
        functools.partial(finish_kernel, len(two), cols_n, sizes),
        operands,
        once,
        [shape_of(shape)] * 2,
        [once[-1]] * 2,
        (1,),
        moved // 4,
        moved,
        "finish",
        scratch=[pltpu.VMEM((3 * shape[1], shape[2]), jnp.float32)],
    )


def shards(ainv, panels, pattern, coupling, dinv):
    rows_n = lax.axis_size("prow")
    cols_n = lax.axis_size("pcol")
    row = lax.axis_index("prow")
    col = lax.axis_index("pcol")
    local_rows, local_cols = panels.shape[1:]
    part = ainv.shape[1] // rows_n
    ratio = cols_n // rows_n
    blocks_here = local_rows // NB

    flags = lax.dynamic_slice_in_dim(pattern, row * blocks_here, blocks_here, 1)
    mask = jnp.repeat(flags.astype(jnp.float32), NB, axis=1)[:, None, :]
    turned = jnp.swapaxes(panels, 1, 2)

    cut = local_cols // 2
    last_cuts = [(0, cut), (cut, local_cols)]
    partner = row ^ jnp.arange(rows_n, dtype=jnp.int32)

    def columns(matrix, cuts):
        cube = matrix.reshape(matrix.shape[0], cols_n, local_cols)
        kept = [cube[:, :, lo:hi].reshape(matrix.shape[0], -1) for lo, hi in cuts]
        return jnp.concatenate(split(jnp.concatenate(kept, 1).T), 0)

    c_one = columns(coupling[0], [(0, local_cols)])
    c_two = columns(coupling[1], last_cuts)
    c_three = columns(coupling[2], last_cuts)

    def gather(shard):
        return lax.all_gather(shard, "pcol", axis=0, tiled=True).reshape(cols_n, *shard.shape)

    def send(pieces):
        return [exchange(p, "prow", rows_n, s + 1) for s, p in enumerate(pieces)]

    def to_columns(groups):
        return lax.all_to_all(negative_sums(order, groups, cols_n), "pcol", 0, 0)

    def to_rows(*values):
        pieces = relay(order, partner, values)
        return [pieces[0]] + send(pieces[1:])

    def share(value):
        return [value] + [exchange(value, "prow", rows_n, s) for s in range(1, rows_n)]

    first, second, third = coupling[0], coupling[1], coupling[2]
    start = col * local_cols

    def own_rows(matrix):
        return lax.dynamic_slice_in_dim(matrix, start, local_cols, 0)

    def own_cols(matrix):
        return lax.dynamic_slice_in_dim(matrix, start, local_cols, 1)

    bridge = second - matmul(first, third)
    d0 = own_rows(dinv[0])
    d1 = own_rows(dinv[1])
    k0 = tdot(own_cols(first), dinv[0])
    k1 = tdot(own_cols(bridge), dinv[0])
    k2 = tdot(own_cols(third), dinv[1])
    base_cross = jnp.stack(
        [-matmul(d0, first), -matmul(d0, bridge), matmul(k0, bridge) - matmul(d1, third)], 0
    )
    base_diag = jnp.stack(
        [d0, d1 + matmul(k0, first), own_rows(dinv[2]) + matmul(k1, bridge) + matmul(k2, third)], 0
    )

    order = Order()
    shard = masked(order, turned, mask, 0, 0, local_cols, [])
    g0 = gather(shard)
    inverse = prepared(order, ainv, partner, rows_n, part)

    early_work = [c_one, c_two, c_three, base_cross, base_diag]
    early_work = [c_one, c_two, c_three, base_cross, base_diag]
    early_work = [c_one, c_two, c_three, base_cross, base_diag]
    shard = masked(order, turned, mask, 1, 0, local_cols, [g0] + early_work)
    g1 = gather(shard)
    f0, sent = products(order, g0, inverse, 0, rows_n)
    s0 = [sent[0]] + send(sent[1:])
    pre1 = elimination(order, [(c_one, f0)], [cols_n * local_cols])

    shard = masked(order, turned, mask, 2, 0, local_cols, [g1])
    g2 = gather(shard)
    f1, sent = products(order, g1, inverse, 0, rows_n, pre1[0])
    s1 = [sent[0]] + send(sent[1:])
    m0 = to_columns([s0])
    pre2 = elimination(
        order, [(c_two, f0), (c_three, f1)], [cols_n * (hi - lo) for lo, hi in last_cuts]
    )

    f2, sent = products(order, g2, inverse, 0, rows_n, pre2[0], (0, 2), s1[1:])
    s2 = [sent[0]] + send(sent[1:])
    m0 = to_rows(m0)
    m1 = to_columns([s1])
    f3, sent = products(order, g2, inverse, 0, rows_n, pre2[1], (1, 2))
    s3 = [sent[0]] + send(sent[1:])
    whole = assembled(order, partner, m0, 0, turned.shape)
    m2 = to_columns([s2])
    m1 = to_rows(m1)
    m3 = to_columns([s3])
    whole = assembled(order, partner, m1, 1, turned.shape, whole)
    m23 = to_rows(m2, m3)
    columns_n, begin, pair = cols_n * local_cols, cols_n * cut, 2 * local_cols
    one = inner_products(
        order, whole, 0, 2, [f0, f1, f2, f3],
        [(0, 0, local_cols), (local_cols, 0, pair)]
        + [(local_cols + pair, c, pair) for c in (0, begin)],
        (local_cols + 2 * pair, columns_n),
    )
    one = share(one)
    whole = assembled(order, partner, m23, 2, turned.shape, whole)
    two = inner_products(
        order, whole, 2, 1, [f2, f3], [(0, c, local_cols) for c in (0, begin)],
        (local_cols, columns_n),
    )
    two = share(two)
    one = negative_sums(order, [one], 1)[0]
    cross, diag = finish(
        order, one, two, base_cross, base_diag, cols_n, (cut, local_cols - cut)
    )
    return (jnp.swapaxes(whole, 1, 2), cross, diag)


def solution(mesh):
    placed = (P("prow", "pcol"), P(None, "prow", "pcol"), P(), P(), P())
    return jax.shard_map(
        shards,
        mesh=mesh,
        in_specs=placed,
        out_specs=(P(None, "prow", "pcol"), P(None, "pcol", None), P(None, "pcol", None)),
        check_vma=False,
    )
```

```python
import functools

import jax
import jax.numpy as jnp
from jax import lax
from jax.experimental import pallas as pl
from jax.experimental.pallas import tpu as pltpu
from jax.sharding import PartitionSpec as P

NB = 128
MIB = 1024 * 1024

precise = lax.Precision.HIGHEST


def matmul(left, right):
    return jnp.dot(left, right, precision=precise, preferred_element_type=jnp.float32)


def tdot(left, right):
    return lax.dot_general(
        left, right, (((0,), (0,)), ((), ())), precision=precise, preferred_element_type=jnp.float32
    )


def tile_of(size, wanted):
    return wanted if size % wanted == 0 else size


def split(values):
    high = lax.reduce_precision(values, exponent_bits=8, mantissa_bits=7)
    return high.astype(jnp.bfloat16), (values - high).astype(jnp.bfloat16)


def split_here(values):
    high = values.astype(jnp.bfloat16)
    return high, (values - high.astype(jnp.float32)).astype(jnp.bfloat16)


def triple_dot(left, right_high, right_low, contract=(1, 0)):
    dims = (((contract[0],), (contract[1],)), ((), ()))
    rows = left.shape[0] // 2
    wide = lax.dot_general(left, right_high, dims, preferred_element_type=jnp.float32)
    cross = lax.dot_general(left[:rows], right_low, dims, preferred_element_type=jnp.float32)
    return wide[:rows] + wide[rows:] + cross


def exchange(value, axis, size, step):
    return lax.ppermute(value, axis, [(i, i ^ step) for i in range(size)])


class Order:
    def __init__(self):
        self.last = None

    def __call__(self, kernel, operands, in_specs, out_shape, out_specs, grid, flops, moved,
                 name, scratch=(), limit=56, prefetch=(), extra=(), aliases=None):
        tokens = list(extra) + ([] if self.last is None else [self.last])
        skip = len(prefetch) + len(operands)

        def body(*refs):
            kernel(*refs[:skip], *refs[skip + len(tokens):])

        got = pl.pallas_call(
            body,
            out_shape=out_shape,
            grid_spec=pltpu.PrefetchScalarGridSpec(
                num_scalar_prefetch=len(prefetch),
                grid=grid,
                in_specs=list(in_specs) + [pl.BlockSpec(memory_space=pl.ANY)] * len(tokens),
                out_specs=out_specs,
                scratch_shapes=list(scratch),
            ),
            compiler_params=pltpu.CompilerParams(vmem_limit_bytes=limit * MIB),
            cost_estimate=pl.CostEstimate(
                flops=flops // 16, bytes_accessed=moved // 16, transcendentals=0
            ),
            input_output_aliases=aliases or {},
            name=name,
        )(*prefetch, *operands, *tokens)
        self.last = got[0] if isinstance(got, (tuple, list)) else got
        return got


def shape_of(shape, dtype=jnp.float32):
    return jax.ShapeDtypeStruct(shape, dtype)


def mask_kernel(panel_ref, mask_ref, out_ref):
    out_ref[...] = panel_ref[0] * mask_ref[0]


def masked(order, panels, mask, j, lo, hi, extra):
    rows = panels.shape[2]
    count = hi - lo
    return order(
        mask_kernel,
        [panels, mask],
        [
            pl.BlockSpec((1, count, rows), lambda i: (j, lo // count, 0)),
            pl.BlockSpec((1, 1, rows), lambda i: (j, 0, 0)),
        ],
        shape_of((count, rows)),
        pl.BlockSpec((count, rows), lambda i: (0, 0)),
        (1,),
        count * rows,
        8 * count * rows,
        "masked",
        extra=extra,
    )


def prepare_kernel(partner_ref, a_ref, high_ref, low_ref):
    high_ref[0], low_ref[0] = split_here(a_ref[...])


def prepared(order, ainv, partner, count, part):
    rows = ainv.shape[0]
    if part % 128:
        pieces = [
            split(lax.dynamic_slice_in_dim(ainv, partner[s] * part, part, 1)) for s in range(count)
        ]
        return jnp.stack([p[0] for p in pieces], 0), jnp.stack([p[1] for p in pieces], 0)
    tile = tile_of(rows, 1024)
    shape = shape_of((count, rows, part), jnp.bfloat16)
    spec = pl.BlockSpec((1, tile, part), lambda s, i, partner: (s, i, 0))
    return order(
        prepare_kernel,
        [ainv],
        [pl.BlockSpec((tile, part), lambda s, i, partner: (i, partner[s]))],
        (shape, shape),
        (spec, spec),
        (count, rows // tile),
        4 * ainv.size,
        8 * ainv.size,
        "prepared",
        prefetch=[partner],
    )


def product_kernel(count, steps, with_pre, with_split, *refs):
    refs = list(refs)
    s, k = pl.program_id(0), pl.program_id(1)
    if with_split:
        gathered_ref = refs.pop(0)
        pre_ref = refs.pop(0) if with_pre else None
        a_high_ref, a_low_ref = refs.pop(0), refs.pop(0)
        factor_ref = refs.pop(0)
        rows, depth = gathered_ref.shape
        here = pl.ds(pl.multiple_of(k * depth, depth), depth)

        @pl.when(s == 0)
        def _():
            strip = 16

            @pl.loop(0, rows // strip)
            def _(i):
                first = pl.multiple_of(i * strip, strip)
                values = gathered_ref[pl.ds(first, strip), :]
                if with_pre:
                    values = values - pre_ref[pl.ds(first, strip), :]
                high, low = split_here(values)
                factor_ref[pl.ds(first, strip), here] = high
                factor_ref[pl.ds(pl.multiple_of(first + rows, strip), strip), here] = low

        factor = factor_ref[:, here]
    else:
        factor_ref, a_high_ref, a_low_ref = refs[:3]
        refs = refs[3:]
        factor = factor_ref[...]
    outs, total_ref = refs[:count], refs[count]
    value = triple_dot(factor, a_high_ref[0], a_low_ref[0])

    @pl.when(k == 0)
    def _():
        total_ref[...] = value

    @pl.when(k > 0)
    def _():
        total_ref[...] += value

    for i in range(count):
        @pl.when((s == i) & (k == steps - 1))
        def _():
            outs[i][...] = total_ref[...]


def products(order, factor, inverse, first, last, pre=None):
    with_split = factor.dtype == jnp.float32
    a_high, a_low = inverse
    count = last - first
    part = a_high.shape[2]
    rows, length = factor.shape
    rows = rows if with_split else rows // 2
    depth = tile_of(length, 2048)
    steps = length // depth
    a_spec = pl.BlockSpec((1, depth, part), lambda s, k: (s + first, k, 0))
    out_shape = [shape_of((rows, part))] * count
    out_specs = [pl.BlockSpec((rows, part), lambda s, k: (0, 0))] * count
    if with_split:
        operands = [factor] + ([] if pre is None else [pre]) + [a_high, a_low]
        once = pl.BlockSpec((rows, depth), lambda s, k: (0, jnp.where(s == 0, k, steps - 1)))
        in_specs = [once] * (len(operands) - 2) + [a_spec, a_spec]
        out_shape = [shape_of((2 * rows, length), jnp.bfloat16)] + out_shape
        out_specs = [pl.BlockSpec((2 * rows, length), lambda s, k: (0, 0))] + out_specs
    else:
        operands = [factor, a_high, a_low]
        in_specs = [pl.BlockSpec((2 * rows, depth), lambda s, k: (0, k)), a_spec, a_spec]
    got = order(
        functools.partial(product_kernel, count, steps, pre is not None, with_split),
        operands,
        in_specs,
        out_shape,
        out_specs,
        (count, steps),
        6 * rows * length * part * count,
        4 * length * part * count + 8 * rows * length,
        "products",
        scratch=[pltpu.VMEM((rows, part), jnp.float32)],
    )
    if with_split:
        return got[0], list(got[1:])
    return factor, list(got)


def elimination_kernel(sources, sizes, *refs):
    value = None
    for i in range(sources):
        coupled, factor_ref = refs[2 * i][...], refs[2 * i + 1]
        depth = factor_ref.shape[0] // 2
        term = triple_dot(coupled, factor_ref[:depth, :], factor_ref[depth:, :])
        value = term if value is None else value + term
    start = 0
    for ref, size in zip(refs[2 * sources :], sizes):
        ref[...] = value[start : start + size]
        start += size


def elimination(order, pairs, sizes):
    operands = [value for pair in pairs for value in pair]
    rows, depth = pairs[0][0].shape[0] // 2, pairs[0][0].shape[1]
    length = pairs[0][1].shape[1]
    tile = tile_of(length, 512)
    left = pl.BlockSpec((2 * rows, depth), lambda i: (0, 0))
    right = pl.BlockSpec((2 * depth, tile), lambda i: (0, i))
    return order(
        functools.partial(elimination_kernel, len(pairs), sizes),
        operands,
        [left, right] * len(pairs),
        [shape_of((size, length)) for size in sizes],
        [pl.BlockSpec((size, tile), lambda i: (0, i)) for size in sizes],
        (length // tile,),
        6 * rows * depth * length * len(pairs),
        4 * length * (rows + depth * len(pairs)),
        "elimination",
    )


def sum_kernel(shares, *refs):
    out = refs[-1]
    start = 0
    for i in range(0, len(refs) - 1, shares):
        value = refs[i][...]
        for ref in refs[i + 1 : i + shares]:
            value = value + ref[...]
        out[0, start : start + value.shape[0], :] = -value
        start += value.shape[0]


def negative_sums(order, groups, cols_n):
    flat = [value for group in groups for value in group]
    width = flat[0].shape[1]
    counts = [group[0].shape[0] // cols_n for group in groups]
    shape = (cols_n, sum(counts), width)
    return order(
        functools.partial(sum_kernel, len(groups[0])),
        flat,
        [pl.BlockSpec((v.shape[0] // cols_n, width), lambda i: (i, 0)) for v in flat],
        shape_of(shape),
        pl.BlockSpec((1, sum(counts), width), lambda i: (i, 0, 0)),
        (cols_n,),
        sum(v.size for v in flat),
        4 * sum(v.size for v in flat),
        "negative_sums",
    )


def relay_kernel(*refs):
    start = 0
    for ref in refs[:-1]:
        refs[-1][:, start : start + ref.shape[1], :] = ref[...]
        start += ref.shape[1]


def relay(order, *values):
    outer, _, width = values[0].shape
    counts = [v.shape[1] for v in values]
    half = outer // 2
    return order(
        relay_kernel,
        list(values),
        [pl.BlockSpec((half, n, width), lambda i: (i, 0, 0)) for n in counts],
        shape_of((outer, sum(counts), width)),
        pl.BlockSpec((half, sum(counts), width), lambda i: (i, 0, 0)),
        (2,),
        sum(v.size for v in values),
        8 * sum(v.size for v in values),
        "relay",
    )


def assembly_kernel(in_ref, *refs):
    out_ref = refs[-1]
    outer, inner, _, part = in_ref.shape
    for a in range(inner):
        for q in range(outer):
            out_ref[0, :, pl.ds((a * outer + q) * part, part)] = in_ref[q, a]


def assembled(order, value, j, shape, whole=None):
    operands = [value] + ([] if whole is None else [whole])
    return order(
        assembly_kernel,
        operands,
        [pl.BlockSpec(value.shape, lambda i: (0, 0, 0, 0))]
        + [pl.BlockSpec(memory_space=pl.ANY)] * (len(operands) - 1),
        shape_of(shape),
        pl.BlockSpec((1, *shape[1:]), lambda i: (j, 0, 0)),
        (1,),
        value.size,
        8 * value.size,
        "assembled",
        aliases={} if whole is None else {1: 0},
    )


def inner_kernel(terms, *refs):
    out = refs[-1]

    @pl.when(pl.program_id(0) == 0)
    def _():
        out[...] = jnp.zeros_like(out)

    stacked = jnp.concatenate(split_here(-refs[0][0]), 0)
    for right, (row, column) in zip(refs[1:-1], terms):
        half = right.shape[0] // 2
        value = triple_dot(stacked, right[:half], right[half:], (1, 1))
        out[row : row + value.shape[0], column : column + half] += value


def inner_products(order, whole, j, rights, terms, shape, extra=()):
    _, count, length = whole.shape
    depth = tile_of(length, 1024)
    return order(
        functools.partial(inner_kernel, terms),
        [whole] + list(rights),
        [pl.BlockSpec((1, count, depth), lambda k: (j, 0, k))]
        + [pl.BlockSpec((v.shape[0], depth), lambda k: (0, k)) for v in rights],
        shape_of(shape),
        pl.BlockSpec(shape, lambda k: (0, 0)),
        (length // depth,),
        6 * shape[0] * shape[1] * length,
        sum(2 * v.size for v in rights),
        "inner_products",
        extra=extra,
    )


def finish_kernel(shares, cols_n, sizes, *refs):
    def total(first):
        value = refs[first][...]
        for ref in refs[first + 1 : first + shares]:
            value = value + ref[...]
        return value

    one, two, three = (total(shares * i) for i in range(3))
    base_cross, base_diag, cross, diag, place = refs[3 * shares :]
    wide = sum(sizes)
    cut = cols_n * sizes[0]
    place[:wide, :] = one[2 * wide :]
    place[wide : 2 * wide, :] = two[wide:]
    place[2 * wide :, :] = three

    def put(out, base, i, row):
        for c in range(cols_n):
            for start, first, size in ((0, 0, sizes[0]), (sizes[0], cut, sizes[1])):
                to = pl.ds(c * wide + start, size)
                out[i, :, to] = base[i, :, to] + place[row : row + wide, pl.ds(first + c * size, size)]

    diag[0] = base_diag[0] + one[:wide]
    cross[0] = base_cross[0] + one[wide : 2 * wide]
    diag[1] = base_diag[1] + two[:wide]
    put(cross, base_cross, 1, 0)
    put(cross, base_cross, 2, wide)
    put(diag, base_diag, 2, 2 * wide)


def finish(order, one, two, three, base_cross, base_diag, cols_n, sizes):
    operands = one + two + three + [base_cross, base_diag]
    shape = base_cross.shape
    once = [pl.BlockSpec(v.shape, lambda i, n=v.ndim: (0,) * n) for v in operands]
    moved = 4 * sum(v.size for v in operands)
    return order(
        functools.partial(finish_kernel, len(one), cols_n, sizes),
        operands,
        once,
        [shape_of(shape)] * 2,
        [once[-1]] * 2,
        (1,),
        moved // 4,
        moved,
        "finish",
        scratch=[pltpu.VMEM((3 * shape[1], shape[2]), jnp.float32)],
    )


def shards(ainv, panels, pattern, coupling, dinv):
    rows_n = lax.axis_size("prow")
    cols_n = lax.axis_size("pcol")
    row = lax.axis_index("prow")
    col = lax.axis_index("pcol")
    local_rows, local_cols = panels.shape[1:]
    part = ainv.shape[1] // rows_n
    ratio = cols_n // rows_n
    blocks_here = local_rows // NB

    flags = lax.dynamic_slice_in_dim(pattern, row * blocks_here, blocks_here, 1)
    mask = jnp.repeat(flags.astype(jnp.float32), NB, axis=1)[:, None, :]
    turned = jnp.swapaxes(panels, 1, 2)

    cut = local_cols * 3 // 4
    chunks = [(0, 0, local_cols), (1, 0, local_cols), (2, 0, cut), (2, cut, local_cols)]
    last_cuts = [(0, cut), (cut, local_cols)]
    partner = row ^ jnp.arange(rows_n, dtype=jnp.int32)

    def columns(matrix, cuts):
        cube = matrix.reshape(matrix.shape[0], cols_n, local_cols)
        kept = [cube[:, :, lo:hi].reshape(matrix.shape[0], -1) for lo, hi in cuts]
        return jnp.concatenate(split(jnp.concatenate(kept, 1).T), 0)

    c_one = columns(coupling[0], [(0, local_cols)])
    c_two = columns(coupling[1], last_cuts)
    c_three = columns(coupling[2], last_cuts)

    def gather(shard):
        return lax.all_gather(shard, "pcol", axis=0, tiled=True)

    def send(pieces):
        return [exchange(p, "prow", rows_n, s + 1) for s, p in enumerate(pieces)]

    def to_columns(groups):
        return lax.all_to_all(negative_sums(order, groups, cols_n), "pcol", 0, 0)

    def to_rows(value):
        count = value.shape[1]
        value = value.reshape(rows_n, ratio * count, part)
        value = lax.all_to_all(value, "prow", 0, 0)
        return value.reshape(rows_n, ratio, count, part)

    def share(value):
        return [value] + [exchange(value, "prow", rows_n, s) for s in range(1, rows_n)]

    first, second, third = coupling[0], coupling[1], coupling[2]
    start = col * local_cols

    def own_rows(matrix):
        return lax.dynamic_slice_in_dim(matrix, start, local_cols, 0)

    def own_cols(matrix):
        return lax.dynamic_slice_in_dim(matrix, start, local_cols, 1)

    bridge = second - matmul(first, third)
    d0 = own_rows(dinv[0])
    d1 = own_rows(dinv[1])
    k0 = tdot(own_cols(first), dinv[0])
    k1 = tdot(own_cols(bridge), dinv[0])
    k2 = tdot(own_cols(third), dinv[1])
    base_cross = jnp.stack(
        [-matmul(d0, first), -matmul(d0, bridge), matmul(k0, bridge) - matmul(d1, third)], 0
    )
    base_diag = jnp.stack(
        [d0, d1 + matmul(k0, first), own_rows(dinv[2]) + matmul(k1, bridge) + matmul(k2, third)], 0
    )

    order = Order()
    shard = masked(order, turned, mask, *chunks[0], [])
    g0 = gather(shard)
    inverse = prepared(order, ainv, partner, rows_n, part)

    early_work = [c_one, c_two, c_three, base_cross, base_diag]
    early_work = [c_one, c_two, c_three, base_cross, base_diag]
    shard = masked(order, turned, mask, *chunks[1], [g0] + early_work)
    g1 = gather(shard)
    f0, sent = products(order, g0, inverse, 0, rows_n)
    s0 = [sent[0]] + send(sent[1:])
    pre1 = elimination(order, [(c_one, f0)], [cols_n * local_cols])

    shard = masked(order, turned, mask, *chunks[2], [g1])
    g2 = gather(shard)
    f1, sent = products(order, g1, inverse, 0, rows_n, pre1[0])
    s1 = [sent[0]] + send(sent[1:])
    m0 = to_columns([s0])
    pre2 = elimination(
        order, [(c_two, f0), (c_three, f1)], [cols_n * (hi - lo) for lo, hi in last_cuts]
    )

    shard = masked(order, turned, mask, *chunks[3], [g2])
    g3 = gather(shard)
    f2, sent = products(order, g2, inverse, 0, rows_n, pre2[0])
    s2 = [sent[0]] + send(sent[1:])
    m0 = to_rows(relay(order, m0))
    m1 = to_columns([s1])

    f3, sent = products(order, g3, inverse, 1, rows_n, pre2[1])
    s3 = send(sent)
    whole = assembled(order, m0, 0, turned.shape)
    m1 = to_rows(relay(order, m1))
    columns_n = cols_n * local_cols
    begin = cols_n * cut
    last = [(0, 0), (0, begin)]
    one = inner_products(
        order, whole, 0, [f0, f1, f2, f3],
        [(0, 0), (local_cols, 0)] + [(2 * local_cols, c) for _, c in last],
        (3 * local_cols, columns_n),
    )
    one = share(one)
    m2 = to_columns([s2])
    _, own3 = products(order, f3, inverse, 0, 1)
    m3 = to_columns([own3 + s3])
    whole = assembled(order, m1, 1, turned.shape, whole)
    two = inner_products(
        order, whole, 1, [f1, f2, f3], [(0, 0)] + [(local_cols, c) for _, c in last],
        (2 * local_cols, columns_n),
    )
    two = share(two)
    m23 = to_rows(relay(order, m2, m3))
    whole = assembled(order, m23, 2, turned.shape, whole)
    three = inner_products(
        order, whole, 2, [f2, f3], last, (local_cols, columns_n), one[1:]
    )
    three = share(three)
    cross, diag = finish(
        order, one, two, three, base_cross, base_diag, cols_n, (cut, local_cols - cut)
    )
    return (jnp.swapaxes(whole, 1, 2), cross, diag)


def solution(mesh):
    placed = (P("prow", "pcol"), P(None, "prow", "pcol"), P(), P(), P())
    return jax.shard_map(
        shards,
        mesh=mesh,
        in_specs=placed,
        out_specs=(P(None, "prow", "pcol"), P(None, "pcol", None), P(None, "pcol", None)),
        check_vma=False,
    )
```
